32 devices in a mesh: node: 8 (over z, core), feat: 4 (over y, x).
Axes of the slice: x: 2, y: 2, z: 4, core: 2. Of those that a mesh axis runs over, the one named last changes fastest.
Arguments:
- x_feat: bfloat16 [512, 32768], P('feat', 'node'), may hold values from -6 to 6
- weight: bfloat16 [512, 512], P('feat'), may hold values from -1 to 1
- out_grad: bfloat16 [512, 32768], P('feat', 'node'), may hold values from -12 to 12
- tile_rows: int32 [960], P('node'), may hold values from 0 to 31, as said below
- tile_cols: int32 [960], P('node'), may hold values from 0 to 255, as said below
- tile_masks: int32 [960, 128, 128], P('node'), may hold values from 0 to 1
Outputs:
- activ: bfloat16 [512, 32768], P('feat', 'node')
- x_grad: bfloat16 [512, 32768], P('feat', 'node')
- weight_grad: float32 [512, 512], P('feat')
The draws below stay inside these ranges and needn't reach their ends.
Inputs may be any that keep to these rules, and one draw needn't show every extreme that they name: `tile_rows`: each node shard's first 32 tiles are its row blocks 0 to 31 in order, each with its own block as column block. `tile_cols`: the tiles of one node shard read at most 8 distinct column blocks held by any one other node shard; in every draw some node shard reads exactly 8 blocks of some other.
All inputs are finite; a program needn't handle non-finite values.
Results may differ from the reference program's by a relative error of at most 0.013.
Values may be sent and summed in bfloat16 or wider, within the bound.
A program may use at most 128 MiB of HBM per device.

```python
from functools import partial
import jax
import jax.numpy as jnp
from jax import lax

F = 512
H = 512
B = 128
BLK_DEV = 32
CAP = 8
NODE_SHARDS = 8
TILE_DEV = 120
BLOCKS = 256
NODES = 32768
TILES = 960


def layout(key):
    shards = NODE_SHARDS
    subkeys = jax.random.split(key, 8)
    counts = jax.random.randint(subkeys[0], (shards, shards), 1, CAP + 1)
    heavy_dst = jax.random.randint(subkeys[1], (shards, 1), 0, 4) == 0
    counts = jnp.where(heavy_dst, CAP, counts)
    full_dst = jax.random.randint(subkeys[2], (), 0, shards)
    full_src = (full_dst + 1 + jax.random.randint(subkeys[3], (), 0, shards - 1)) % shards
    counts = counts.at[full_dst, full_src].set(CAP)
    scores = jax.random.randint(subkeys[4], (shards, shards, BLK_DEV), 0, 1 << 20) * BLK_DEV + jnp.arange(BLK_DEV, dtype=jnp.int32)
    picked = jnp.argsort(scores, axis=-1, stable=True)[..., :CAP].astype(jnp.int32)
    slot_index = jnp.arange(TILE_DEV, dtype=jnp.int32)[None, :]
    shard_index = jnp.arange(shards, dtype=jnp.int32)[:, None]
    offset = jnp.clip(slot_index - BLK_DEV, 0, (shards - 1) * CAP - 1)
    peer_shard = (shard_index + 1 + offset // CAP) % shards
    within = offset % CAP
    is_live = within < counts[shard_index, peer_shard]
    remote_col = peer_shard * BLK_DEV + picked[shard_index, peer_shard, within]
    local_col = shard_index * BLK_DEV + jax.random.randint(subkeys[5], (shards, TILE_DEV), 0, BLK_DEV)
    is_remote = (slot_index >= BLK_DEV) & (slot_index < BLK_DEV + (shards - 1) * CAP) & is_live
    diagonal = slot_index < BLK_DEV
    tile_col = jnp.where(diagonal, shard_index * BLK_DEV + slot_index, jnp.where(is_remote, remote_col, local_col))
    row_draw = jnp.minimum(jax.random.randint(subkeys[6], (shards, TILE_DEV), 0, BLK_DEV), jax.random.randint(subkeys[7], (shards, TILE_DEV), 0, BLK_DEV))
    tile_row = jnp.where(diagonal, slot_index + 0 * shard_index, row_draw)
    return (tile_row.reshape(TILES).astype(jnp.int32), tile_col.reshape(TILES).astype(jnp.int32))


def draw_tile_rows(key, part):
    tile_row, tile_col = layout(key)
    return tile_row


def draw_tile_cols(key, part):
    tile_row, tile_col = layout(key)
    return tile_col


def draw_tile_masks(key, part):
    key = jax.random.fold_in(key, 11)
    halves = jax.random.split(key, 2)
    density = jax.random.randint(halves[0], (TILES, 1, 1), 10, 61)
    sampled = jax.random.randint(halves[1], (TILES, B, B), 0, 1000)
    return (sampled < density).astype(jnp.int32)


def levels(stream_key, extent, pieces, smallest, high):
    def one(position, parts):
        steps = jax.random.uniform(jax.random.fold_in(jax.random.fold_in(stream_key, 6), position), (parts,), jnp.float32, smallest / len(pieces), high / len(pieces))
        return jnp.repeat(jnp.exp(steps), extent[position] // parts).reshape((-1,) + (1,) * (len(extent) - position - 1))

    level = one(*pieces[0])
    for cut in pieces[1:]:
        level = level * one(*cut)
    return level


def noise(stream_key, dims, width, reach, pieces=(), kind=jnp.bfloat16):
    entries = width * jax.random.normal(stream_key, dims, jnp.float32)
    if pieces:
        entries = entries * levels(stream_key, dims, pieces, -0.22, 0.18)
    return jnp.clip(entries, -reach, reach).astype(kind)


def setup_inputs(seed: int = 0) -> dict:
    keys = jax.random.split(jax.random.key(seed), 7)
    x_feat = noise(keys[0], (F, NODES), 1.0, 6.0, ((0, 4), (1, 8)))
    weight = noise(keys[1], (F, H), (F // 16) ** -0.5, 1.0, ((0, 4),))
    out_grad = noise(keys[2], (H, NODES), 2.0, 12.0, ((0, 4), (1, 8)))
    tile_rows = draw_tile_rows(jax.random.fold_in(keys[6], 71), 0)
    tile_cols = draw_tile_cols(jax.random.fold_in(keys[6], 71), 0)
    tile_masks = draw_tile_masks(jax.random.fold_in(keys[6], 71), 0)
    return dict(x_feat=x_feat, weight=weight, out_grad=out_grad, tile_rows=tile_rows, tile_cols=tile_cols, tile_masks=tile_masks)


def silu_slope(value):
    sig = jax.nn.sigmoid(value)
    return sig * (1.0 + value * (1.0 - sig))


def aggregate_shard(packed, x_blocks):
    tile_row, tile_col, tile_mask, shard_index = packed
    edge_values = tile_mask.astype(jnp.float32)
    row_onehot = (tile_row[None, :] == jnp.arange(BLK_DEV, dtype=jnp.int32)[:, None]).astype(jnp.float32)
    degree = 1.0 + jnp.dot(row_onehot, jnp.sum(edge_values, axis=2), precision=lax.Precision.HIGHEST)
    source = jnp.take(x_blocks, tile_col, axis=1).astype(jnp.float32)
    tile_terms = jnp.einsum('ftc,trc->ftr', source, edge_values, precision=lax.Precision.HIGHEST)
    summed = jnp.einsum('bt,ftr->fbr', row_onehot, tile_terms, precision=lax.Precision.HIGHEST)
    own_rows = lax.dynamic_slice_in_dim(x_blocks, (shard_index * BLK_DEV).astype(jnp.int32), BLK_DEV, 1).astype(jnp.float32)
    mixed = ((own_rows + summed) / degree[None]).astype(jnp.bfloat16)
    return mixed, degree


def spread_shard(running, packed):
    tile_row, tile_col, tile_mask, scaled_shard = packed
    edge_values = tile_mask.astype(jnp.float32)
    source = jnp.take(scaled_shard, tile_row, axis=1).astype(jnp.float32)
    contrib = jnp.einsum('ftr,trc->ftc', source, edge_values, precision=lax.Precision.HIGHEST)
    return running.at[:, tile_col, :].add(contrib), None


def reference(x_feat, weight, out_grad, tile_rows, tile_cols, tile_masks):
    x_blocks = x_feat.reshape(F, BLOCKS, B)
    row_sets = tile_rows.reshape(NODE_SHARDS, TILE_DEV)
    col_sets = tile_cols.reshape(NODE_SHARDS, TILE_DEV)
    mask_sets = tile_masks.reshape(NODE_SHARDS, TILE_DEV, B, B)
    shard_ids = jnp.arange(NODE_SHARDS, dtype=jnp.int32)
    mixed, degree = lax.map(partial(aggregate_shard, x_blocks=x_blocks), (row_sets, col_sets, mask_sets, shard_ids))
    aggregated = jnp.transpose(mixed, (1, 0, 2, 3)).reshape(F, NODES)
    degrees = degree.reshape(NODES)
    preact = jnp.dot(weight.T, aggregated, preferred_element_type=jnp.float32)
    activ = jax.nn.silu(preact).astype(jnp.bfloat16)
    masked_grad = (out_grad.astype(jnp.float32) * silu_slope(preact)).astype(jnp.bfloat16)
    hidden_grad = jnp.dot(weight, masked_grad, preferred_element_type=jnp.float32).astype(jnp.bfloat16)
    weight_grad = jnp.dot(aggregated, masked_grad.T, preferred_element_type=jnp.float32) * (NODES ** -0.5)
    scaled = (hidden_grad.astype(jnp.float32) / degrees[None, :]).astype(jnp.bfloat16)
    scaled_sets = jnp.transpose(scaled.reshape(F, NODE_SHARDS, BLK_DEV, B), (1, 0, 2, 3))
    running, unused = lax.scan(spread_shard, jnp.zeros((F, BLOCKS, B), jnp.float32), (row_sets, col_sets, mask_sets, scaled_sets))
    x_grad = (scaled.astype(jnp.float32) + running.reshape(F, NODES)).astype(jnp.bfloat16)
    return activ, x_grad, weight_grad
```

```python
import functools

import jax
import jax.numpy as jnp
from jax import lax
from jax.experimental import pallas as pl
from jax.experimental.pallas import tpu as pltpu
from jax.sharding import PartitionSpec as P

CAP = 8
GROUP = 8
LANES = 128
MESH = pl.DeviceIdType.MESH
VMEM = pltpu.VMEM
SMEM = pltpu.SMEM
ANY = pl.ANY


def spec(space):
    return pl.BlockSpec(memory_space=space)


def params(limit_mib, **more):
    return pltpu.CompilerParams(vmem_limit_bytes=limit_mib << 20, **more)


def plan_kernel(shards, blocks, tiles, cols_ref, need_ref, slot_ref, pos, count):
    me = lax.axis_index("node")

    @pl.loop(0, shards)
    def _(s):
        count[s] = 0
        for k in range(CAP):
            need_ref[s, k] = 0

    @pl.loop(0, tiles)
    def _(t):
        pos[cols_ref[t]] = -1

    @pl.loop(0, tiles)
    def _(t):
        col = cols_ref[t]
        shard = col // blocks
        local = col - shard * blocks

        @pl.when(shard == me)
        def _():
            slot_ref[t] = local

        @pl.when(shard != me)
        def _():
            @pl.when(pos[col] < 0)
            def _():
                fresh = count[shard]
                pos[col] = fresh
                count[shard] = fresh + 1
                need_ref[shard, fresh] = local

            slot_ref[t] = blocks + shard * CAP + pos[col]


def barrier(shards, feats):
    node, feat = lax.axis_index("node"), lax.axis_index("feat")
    sem = pltpu.get_barrier_semaphore()
    for off in range(1, shards):
        pl.semaphore_signal(
            sem, inc=1, device_id=(lax.rem(node + off, shards), feat), device_id_type=MESH
        )
    for off in range(1, feats):
        pl.semaphore_signal(
            sem, inc=1, device_id=(node, lax.rem(feat + off, feats)), device_id_type=MESH
        )
    pl.semaphore_wait(sem, shards - 1 + (feats - 1 if feats else 0))


def ask_kernel(shards, need_ref, asked_ref, send_sem, recv_sem, self_sem):
    node, feat = lax.axis_index("node"), lax.axis_index("feat")
    barrier(shards, 0)
    copies = []
    for off in range(1, shards):
        peer = lax.rem(node + off, shards)
        copy = pltpu.make_async_remote_copy(
            src_ref=need_ref.at[peer], dst_ref=asked_ref.at[node],
            send_sem=send_sem.at[off - 1], recv_sem=recv_sem.at[off - 1],
            device_id=(peer, feat), device_id_type=MESH,
        )
        copy.start()
        copies.append(copy)
    own = pltpu.make_async_copy(need_ref.at[node], asked_ref.at[node], self_sem)
    own.start()
    own.wait()
    for copy in copies:
        copy.wait()


def pick_kernel(shards, asked_ref, x_ref, outbox_ref):
    for s in range(shards):

        @pl.loop(0, CAP)
        def _(k):
            columns = pl.ds(pl.multiple_of(asked_ref[s, k] * LANES, LANES), LANES)
            outbox_ref[s * CAP + k] = x_ref[:, columns]


def fetch_kernel(
    shards, feats, blocks, outbox_ref, x_ref, grad_ref, weight_ref, source_ref,
    cot_ref, full_ref, x_send, x_recv, own_sem, cot_send, cot_recv, w_send, w_recv, self_sem,
):
    node, feat = lax.axis_index("node"), lax.axis_index("feat")
    depth = x_ref.shape[0]
    per_feat = cot_ref.shape[1]
    barrier(shards, feats)
    mine = pl.ds(node * CAP, CAP)
    landing = pl.ds(blocks + node * CAP, CAP)

    copies = []
    for off in range(1, shards):
        peer = lax.rem(node + off, shards)
        copies.append(pltpu.make_async_remote_copy(
            src_ref=outbox_ref.at[pl.ds(peer * CAP, CAP)], dst_ref=source_ref.at[landing],
            send_sem=x_send.at[off - 1], recv_sem=x_recv.at[off - 1],
            device_id=(peer, feat), device_id_type=MESH,
        ))
    rows = pl.ds(pl.multiple_of(feat * depth, depth), depth)
    for off in range(1, feats):
        peer = lax.rem(feat + off, feats)
        columns = pl.ds(pl.multiple_of(peer * per_feat, per_feat), per_feat)
        for src, dst, sent, got in (
            (weight_ref, full_ref.at[rows], w_send, w_recv),
            (grad_ref.at[:, columns], cot_ref.at[rows], cot_send, cot_recv),
        ):
            copies.append(pltpu.make_async_remote_copy(
                src_ref=src, dst_ref=dst, send_sem=sent.at[off - 1], recv_sem=got.at[off - 1],
                device_id=(node, peer), device_id_type=MESH,
            ))
    own = pl.ds(pl.multiple_of(feat * per_feat, per_feat), per_feat)
    copies += [
        pltpu.make_async_copy(weight_ref, full_ref.at[rows], self_sem.at[0]),
        pltpu.make_async_copy(grad_ref.at[:, own], cot_ref.at[rows], self_sem.at[1]),
        pltpu.make_async_copy(outbox_ref.at[mine], source_ref.at[landing], self_sem.at[2]),
    ]
    for b in range(blocks):
        copies.append(pltpu.make_async_copy(
            x_ref.at[:, pl.ds(b * LANES, LANES)], source_ref.at[b], own_sem.at[b]
        ))
    for copy in copies:
        copy.start()
    for copy in copies:
        copy.wait()


def gather_kernel(steps, blocks, rows_ref, slot_ref, source_ref, mask_ref, agg_ref, deg_ref, edge_ref, acc):
    step = pl.program_id(0)
    depth = source_ref.shape[1]
    ones = jnp.ones((16, LANES), jnp.bfloat16)

    def term(g):
        t = step * GROUP + g
        edges = mask_ref[g].astype(jnp.float32).astype(jnp.bfloat16)
        edge_ref[g] = edges
        source = jnp.concatenate([source_ref[slot_ref[t]], ones], axis=0)
        return rows_ref[t], lax.dot_general(
            source, edges, (((1,), (1,)), ((), ())), preferred_element_type=jnp.float32
        )

    @pl.when(step < blocks // GROUP)
    def _():
        for g in range(GROUP):
            row, value = term(g)
            acc[row] = value

    @pl.when(step >= blocks // GROUP)
    def _():
        for g in range(0, GROUP, 2):
            row0, value0 = term(g)
            row1, value1 = term(g + 1)
            acc[row0] += value0
            acc[row1] += value1

    @pl.when(step == steps - 1)
    def _():
        for b in range(blocks):
            degree = 1.0 + acc[b, depth : depth + 1, :]
            mixed = source_ref[b].astype(jnp.float32) + acc[b, :depth, :]
            agg_ref[:, b * LANES : (b + 1) * LANES] = (mixed / degree).astype(jnp.bfloat16)
            deg_ref[b] = degree


def spread_kernel(steps, blocks, rows_ref, slot_ref, hidden_ref, deg_ref, edge_ref, own_ref, terms_ref, acc, scaled):
    step = pl.program_id(0)

    @pl.when(step == 0)
    def _():
        for b in range(blocks):
            value = hidden_ref[:, b * LANES : (b + 1) * LANES].astype(jnp.float32) / deg_ref[b]
            value = value.astype(jnp.bfloat16)
            scaled[b] = value
            acc[b] = value.astype(jnp.float32)
        acc[blocks:] = jnp.zeros_like(acc[blocks:])

    def term(g):
        t = step * GROUP + g
        return slot_ref[t], jnp.dot(
            scaled[rows_ref[t]], edge_ref[g], preferred_element_type=jnp.float32
        )

    for g in range(0, GROUP, 2):
        slot0, value0 = term(g)
        slot1, value1 = term(g + 1)
        acc[slot0] += value0
        acc[slot1] += value1

    @pl.when(step == steps - 1)
    def _():
        own_ref[...] = acc[:blocks]
        terms_ref[...] = acc[blocks:].astype(jnp.bfloat16)


def return_kernel(shards, terms_ref, back_ref, send_sem, recv_sem, self_sem):
    node, feat = lax.axis_index("node"), lax.axis_index("feat")
    barrier(shards, 0)
    copies = []
    for off in range(1, shards):
        peer = lax.rem(node + off, shards)
        copy = pltpu.make_async_remote_copy(
            src_ref=terms_ref.at[pl.ds(peer * CAP, CAP)],
            dst_ref=back_ref.at[pl.ds(node * CAP, CAP)],
            send_sem=send_sem.at[off - 1], recv_sem=recv_sem.at[off - 1],
            device_id=(peer, feat), device_id_type=MESH,
        )
        copy.start()
        copies.append(copy)
    mine = pl.ds(node * CAP, CAP)
    own = pltpu.make_async_copy(terms_ref.at[mine], back_ref.at[mine], self_sem)
    own.start()
    own.wait()
    for copy in copies:
        copy.wait()


def merge_kernel(shards, blocks, asked_ref, own_ref, back_ref, out_ref, acc):
    node = lax.axis_index("node")
    acc[...] = own_ref[...]
    for off in range(1, shards):
        peer = lax.rem(node + off, shards)

        @pl.loop(0, CAP)
        def _(k):
            acc[asked_ref[peer, k]] += back_ref[peer * CAP + k].astype(jnp.float32)

    for b in range(blocks):
        out_ref[:, b * LANES : (b + 1) * LANES] = acc[b].astype(jnp.bfloat16)


def silu_slope(value):
    sig = jax.nn.sigmoid(value)
    return sig * (1.0 + value * (1.0 - sig))


def per_device(shards, feats, x_feat, weight, out_grad, tile_rows, tile_cols, tile_masks):
    depth, local_rows = x_feat.shape
    blocks = local_rows // LANES
    tiles = tile_cols.shape[0]
    hidden = weight.shape[1]
    features = depth * feats
    per_feat = local_rows // feats
    slots = blocks + shards * CAP
    bf16, f32, i32 = jnp.bfloat16, jnp.float32, jnp.int32
    shape = jax.ShapeDtypeStruct
    dma = pltpu.SemaphoreType.DMA
    steps = tiles // GROUP

    need, slot = pl.pallas_call(
        functools.partial(plan_kernel, shards, blocks, tiles),
        out_shape=(shape((shards, LANES), i32), shape((tiles,), i32)),
        in_specs=[spec(SMEM)],
        out_specs=(spec(SMEM), spec(SMEM)),
        scratch_shapes=[SMEM((blocks * shards,), i32), SMEM((shards,), i32)],
    )(tile_cols)

    asked = pl.pallas_call(
        functools.partial(ask_kernel, shards),
        out_shape=shape((shards, 1, LANES), i32),
        in_specs=[spec(VMEM)],
        out_specs=spec(VMEM),
        scratch_shapes=[dma((shards - 1,)), dma((shards - 1,)), dma(())],
        compiler_params=params(16, collective_id=2, has_side_effects=True),
    )(need.reshape(shards, 1, LANES)).reshape(shards, LANES)

    outbox = pl.pallas_call(
        functools.partial(pick_kernel, shards),
        out_shape=shape((shards * CAP, depth, LANES), bf16),
        in_specs=[spec(SMEM), spec(VMEM)],
        out_specs=spec(VMEM),
        compiler_params=params(24),
    )(asked, x_feat)

    source, cotangent_rows, full_weight = pl.pallas_call(
        functools.partial(fetch_kernel, shards, feats, blocks),
        out_shape=(
            shape((slots, depth, LANES), bf16),
            shape((features, per_feat), bf16),
            shape((features, hidden), bf16),
        ),
        in_specs=[spec(ANY)] * 4,
        out_specs=(spec(ANY),) * 3,
        scratch_shapes=[
            dma((shards - 1,)), dma((shards - 1,)), dma((blocks,)),
            dma((feats - 1,)), dma((feats - 1,)), dma((feats - 1,)), dma((feats - 1,)),
            dma((3,)),
        ],
        compiler_params=params(24, collective_id=0, has_side_effects=True),
    )(outbox, x_feat, out_grad, weight)

    whole3 = lambda i, *_: (0, 0, 0)
    whole2 = lambda i, *_: (0, 0)
    by_tile = lambda i, *_: (i, 0, 0)
    aggregated, degree, edges = pl.pallas_call(
        functools.partial(gather_kernel, steps, blocks),
        grid_spec=pltpu.PrefetchScalarGridSpec(
            num_scalar_prefetch=2,
            grid=(steps,),
            in_specs=[
                pl.BlockSpec((slots, depth, LANES), whole3),
                pl.BlockSpec((GROUP, LANES, LANES), by_tile),
            ],
            out_specs=(
                pl.BlockSpec((depth, local_rows), whole2),
                pl.BlockSpec((blocks, 1, LANES), whole3),
                pl.BlockSpec((GROUP, LANES, LANES), by_tile),
            ),
            scratch_shapes=[VMEM((blocks, depth + 16, LANES), f32)],
        ),
        out_shape=(
            shape((depth, local_rows), bf16),
            shape((blocks, 1, LANES), f32),
            shape((tiles, LANES, LANES), bf16),
        ),
        compiler_params=params(40),
    )(tile_rows, slot, source, tile_masks)

    node_rows = lax.all_to_all(aggregated, "feat", split_axis=1, concat_axis=0, tiled=True)
    row_preact = lax.dot_general(
        full_weight, node_rows, (((0,), (0,)), ((), ())), preferred_element_type=f32
    )
    row_activ = jax.nn.silu(row_preact).astype(bf16)
    activ = lax.all_to_all(row_activ, "feat", split_axis=0, concat_axis=1, tiled=True)
    grad_rows = (cotangent_rows.astype(f32) * silu_slope(row_preact)).astype(bf16)
    row_hidden = jnp.dot(full_weight, grad_rows, preferred_element_type=f32).astype(bf16)
    hidden_grad = lax.all_to_all(row_hidden, "feat", split_axis=0, concat_axis=1, tiled=True)
    full_part = lax.dot_general(
        node_rows, grad_rows, (((1,), (1,)), ((), ())), preferred_element_type=f32
    )
    part_grad = lax.psum_scatter(full_part, "feat", scatter_dimension=0, tiled=True)
    weight_grad = lax.psum(part_grad, "node") * (local_rows * shards) ** (-0.5)

    own, terms = pl.pallas_call(
        functools.partial(spread_kernel, steps, blocks),
        grid_spec=pltpu.PrefetchScalarGridSpec(
            num_scalar_prefetch=2,
            grid=(steps,),
            in_specs=[
                pl.BlockSpec((depth, local_rows), whole2),
                pl.BlockSpec((blocks, 1, LANES), whole3),
                pl.BlockSpec((GROUP, LANES, LANES), by_tile),
            ],
            out_specs=(
                pl.BlockSpec((blocks, depth, LANES), whole3),
                pl.BlockSpec((shards * CAP, depth, LANES), whole3),
            ),
            scratch_shapes=[
                VMEM((slots, depth, LANES), f32),
                VMEM((blocks, depth, LANES), bf16),
            ],
        ),
        out_shape=(
            shape((blocks, depth, LANES), f32),
            shape((shards * CAP, depth, LANES), bf16),
        ),
        compiler_params=params(40),
    )(tile_rows, slot, hidden_grad, degree, edges)

    back = pl.pallas_call(
        functools.partial(return_kernel, shards),
        out_shape=shape((shards * CAP, depth, LANES), bf16),
        in_specs=[spec(ANY)],
        out_specs=spec(ANY),
        scratch_shapes=[dma((shards - 1,)), dma((shards - 1,)), dma(())],
        compiler_params=params(24, collective_id=1, has_side_effects=True),
    )(terms)

    x_grad = pl.pallas_call(
        functools.partial(merge_kernel, shards, blocks),
        out_shape=shape((depth, local_rows), bf16),
        in_specs=[spec(SMEM), spec(VMEM), spec(VMEM)],
        out_specs=spec(VMEM),
        scratch_shapes=[VMEM((blocks, depth, LANES), f32)],
        compiler_params=params(32),
    )(asked, own, back)
    return (activ, x_grad, weight_grad)


def solution(mesh):
    placed = (
        P("feat", "node"),
        P("feat", None),
        P("feat", "node"),
        P("node"),
        P("node"),
        P("node", None, None),
    )
    return jax.shard_map(
        functools.partial(per_device, mesh.shape["node"], mesh.shape["feat"]),
        mesh=mesh,
        in_specs=placed,
        out_specs=(P("feat", "node"), P("feat", "node"), P("feat", None)),
        check_vma=False,
    )
```

```python
import functools

import jax
import jax.numpy as jnp
from jax import lax
from jax.experimental import pallas as pl
from jax.experimental.pallas import tpu as pltpu
from jax.sharding import PartitionSpec as P

CAP = 8
GROUP = 8
LANES = 128
MESH = pl.DeviceIdType.MESH
VMEM = pltpu.VMEM
SMEM = pltpu.SMEM
ANY = pl.ANY


def spec(space):
    return pl.BlockSpec(memory_space=space)


def params(limit_mib, **more):
    return pltpu.CompilerParams(vmem_limit_bytes=limit_mib << 20, **more)


def plan_kernel(shards, blocks, tiles, cols_ref, need_ref, slot_ref, pos, count):
    me = lax.axis_index("node")

    @pl.loop(0, shards)
    def _(s):
        count[s] = 0
        for k in range(CAP):
            need_ref[s, k] = 0

    @pl.loop(0, tiles)
    def _(t):
        pos[cols_ref[t]] = -1

    @pl.loop(0, tiles)
    def _(t):
        col = cols_ref[t]
        shard = col // blocks
        local = col - shard * blocks

        @pl.when(shard == me)
        def _():
            slot_ref[t] = local

        @pl.when(shard != me)
        def _():
            @pl.when(pos[col] < 0)
            def _():
                fresh = count[shard]
                pos[col] = fresh
                count[shard] = fresh + 1
                need_ref[shard, fresh] = local

            slot_ref[t] = blocks + shard * CAP + pos[col]


def barrier(shards, feats):
    node, feat = lax.axis_index("node"), lax.axis_index("feat")
    sem = pltpu.get_barrier_semaphore()
    for off in range(1, shards):
        pl.semaphore_signal(
            sem, inc=1, device_id=(lax.rem(node + off, shards), feat), device_id_type=MESH
        )
    for off in range(1, feats):
        pl.semaphore_signal(
            sem, inc=1, device_id=(node, lax.rem(feat + off, feats)), device_id_type=MESH
        )
    pl.semaphore_wait(sem, max(shards - 1, 0) + max(feats - 1, 0))


def ask_kernel(shards, need_ref, asked_ref, send_sem, recv_sem, self_sem):
    node, feat = lax.axis_index("node"), lax.axis_index("feat")
    barrier(shards, 0)
    copies = []
    for off in range(1, shards):
        peer = lax.rem(node + off, shards)
        copy = pltpu.make_async_remote_copy(
            src_ref=need_ref.at[peer], dst_ref=asked_ref.at[node],
            send_sem=send_sem.at[off - 1], recv_sem=recv_sem.at[off - 1],
            device_id=(peer, feat), device_id_type=MESH,
        )
        copy.start()
        copies.append(copy)
    own = pltpu.make_async_copy(need_ref.at[node], asked_ref.at[node], self_sem)
    own.start()
    own.wait()
    for copy in copies:
        copy.wait()


def pick_kernel(shards, asked_ref, x_ref, outbox_ref):
    for s in range(shards):

        @pl.loop(0, CAP)
        def _(k):
            columns = pl.ds(pl.multiple_of(asked_ref[s, k] * LANES, LANES), LANES)
            outbox_ref[s * CAP + k] = x_ref[:, columns]


def fetch_kernel(
    shards, feats, blocks, outbox_ref, x_ref, grad_ref, weight_ref, source_ref,
    cot_ref, full_ref, x_send, x_recv, own_sem, cot_send, cot_recv, w_send, w_recv, self_sem,
):
    node, feat = lax.axis_index("node"), lax.axis_index("feat")
    depth = x_ref.shape[0]
    per_feat = cot_ref.shape[1]
    barrier(shards, feats)
    mine = pl.ds(node * CAP, CAP)
    landing = pl.ds(blocks + node * CAP, CAP)

    copies = []
    for off in range(1, shards):
        peer = lax.rem(node + off, shards)
        copies.append(pltpu.make_async_remote_copy(
            src_ref=outbox_ref.at[pl.ds(peer * CAP, CAP)], dst_ref=source_ref.at[landing],
            send_sem=x_send.at[off - 1], recv_sem=x_recv.at[off - 1],
            device_id=(peer, feat), device_id_type=MESH,
        ))
    rows = pl.ds(pl.multiple_of(feat * depth, depth), depth)
    for off in range(1, feats):
        peer = lax.rem(feat + off, feats)
        columns = pl.ds(pl.multiple_of(peer * per_feat, per_feat), per_feat)
        for src, dst, sent, got in (
            (weight_ref, full_ref.at[rows], w_send, w_recv),
            (grad_ref.at[:, columns], cot_ref.at[rows], cot_send, cot_recv),
        ):
            copies.append(pltpu.make_async_remote_copy(
                src_ref=src, dst_ref=dst, send_sem=sent.at[off - 1], recv_sem=got.at[off - 1],
                device_id=(node, peer), device_id_type=MESH,
            ))
    own = pl.ds(pl.multiple_of(feat * per_feat, per_feat), per_feat)
    copies += [
        pltpu.make_async_copy(weight_ref, full_ref.at[rows], self_sem.at[0]),
        pltpu.make_async_copy(grad_ref.at[:, own], cot_ref.at[rows], self_sem.at[1]),
        pltpu.make_async_copy(outbox_ref.at[mine], source_ref.at[landing], self_sem.at[2]),
    ]
    for b in range(blocks):
        copies.append(pltpu.make_async_copy(
            x_ref.at[:, pl.ds(b * LANES, LANES)], source_ref.at[b], own_sem.at[b]
        ))
    for copy in copies:
        copy.start()
    for copy in copies:
        copy.wait()


def gather_kernel(steps, blocks, rows_ref, slot_ref, source_ref, mask_ref, agg_ref, deg_ref, edge_ref, acc):
    step = pl.program_id(0)
    depth = source_ref.shape[1]
    ones = jnp.ones((16, LANES), jnp.bfloat16)

    def term(g):
        t = step * GROUP + g
        edges = mask_ref[g].astype(jnp.float32).astype(jnp.bfloat16)
        edge_ref[g] = edges
        source = jnp.concatenate([source_ref[slot_ref[t]], ones], axis=0)
        return rows_ref[t], lax.dot_general(
            source, edges, (((1,), (1,)), ((), ())), preferred_element_type=jnp.float32
        )

    @pl.when(step < blocks // GROUP)
    def _():
        for g in range(GROUP):
            row, value = term(g)
            acc[row] = value

    @pl.when(step >= blocks // GROUP)
    def _():
        for g in range(0, GROUP, 2):
            row0, value0 = term(g)
            row1, value1 = term(g + 1)
            acc[row0] += value0
            acc[row1] += value1

    @pl.when(step == steps - 1)
    def _():
        for b in range(blocks):
            degree = 1.0 + acc[b, depth : depth + 1, :]
            mixed = source_ref[b].astype(jnp.float32) + acc[b, :depth, :]
            agg_ref[:, b * LANES : (b + 1) * LANES] = (mixed / degree).astype(jnp.bfloat16)
            deg_ref[b] = degree


def spread_kernel(steps, blocks, rows_ref, slot_ref, hidden_ref, deg_ref, edge_ref, own_ref, terms_ref, acc, scaled):
    step = pl.program_id(0)

    @pl.when(step == 0)
    def _():
        for b in range(blocks):
            value = hidden_ref[:, b * LANES : (b + 1) * LANES].astype(jnp.float32) / deg_ref[b]
            value = value.astype(jnp.bfloat16)
            scaled[b] = value
            acc[b] = value.astype(jnp.float32)
        acc[blocks:] = jnp.zeros_like(acc[blocks:])

    def term(g):
        t = step * GROUP + g
        return slot_ref[t], jnp.dot(
            scaled[rows_ref[t]], edge_ref[g], preferred_element_type=jnp.float32
        )

    for g in range(0, GROUP, 2):
        slot0, value0 = term(g)
        slot1, value1 = term(g + 1)
        acc[slot0] += value0
        acc[slot1] += value1

    @pl.when(step == steps - 1)
    def _():
        own_ref[...] = acc[:blocks]
        terms_ref[...] = acc[blocks:].astype(jnp.bfloat16)


def band(index, size):
    return pl.ds(pl.multiple_of(index * size, size), size)


def swap_kernel(feats, to_columns, src_ref, dst_ref, send_sem, recv_sem, self_sem):
    node, feat = lax.axis_index("node"), lax.axis_index("feat")
    barrier(0, feats)
    depth = min(src_ref.shape[0], dst_ref.shape[0])
    width = min(src_ref.shape[1], dst_ref.shape[1])

    def ends(peer):
        if to_columns:
            return src_ref.at[band(peer, depth)], dst_ref.at[:, band(feat, width)]
        return src_ref.at[:, band(peer, width)], dst_ref.at[band(feat, depth)]

    copies = []
    for off in range(1, feats):
        peer = lax.rem(feat + off, feats)
        src, dst = ends(peer)
        copies.append(pltpu.make_async_remote_copy(
            src_ref=src, dst_ref=dst, send_sem=send_sem.at[off - 1],
            recv_sem=recv_sem.at[off - 1], device_id=(node, peer), device_id_type=MESH,
        ))
    src, dst = ends(feat)
    copies.append(pltpu.make_async_copy(src, dst, self_sem))
    for copy in copies:
        copy.start()
    for copy in copies:
        copy.wait()


def return_kernel(
    shards, feats, scale, terms_ref, rows_ref, part_ref, back_ref, activ_ref, grad_ref,
    feat_in, partial, node_in, reduced, gathered, z_send, z_recv, a_send, a_recv, self_sem,
    p_send, p_recv, q_send, q_recv, r_send, r_recv,
):
    node, feat = lax.axis_index("node"), lax.axis_index("feat")
    depth = activ_ref.shape[0]
    width = rows_ref.shape[1]
    barrier(shards, feats)

    parts = []
    for off in range(1, feats):
        peer = lax.rem(feat + off, feats)
        parts.append(pltpu.make_async_remote_copy(
            src_ref=part_ref.at[peer], dst_ref=feat_in.at[off - 1],
            send_sem=p_send.at[off - 1], recv_sem=p_recv.at[off - 1],
            device_id=(node, peer), device_id_type=MESH,
        ))
    copies = []
    for off in range(1, shards):
        peer = lax.rem(node + off, shards)
        copies.append(pltpu.make_async_remote_copy(
            src_ref=terms_ref.at[pl.ds(peer * CAP, CAP)],
            dst_ref=back_ref.at[pl.ds(node * CAP, CAP)],
            send_sem=z_send.at[off - 1], recv_sem=z_recv.at[off - 1],
            device_id=(peer, feat), device_id_type=MESH,
        ))
    for off in range(1, feats):
        peer = lax.rem(feat + off, feats)
        copies.append(pltpu.make_async_remote_copy(
            src_ref=rows_ref.at[band(peer, depth)], dst_ref=activ_ref.at[:, band(feat, width)],
            send_sem=a_send.at[off - 1], recv_sem=a_recv.at[off - 1],
            device_id=(node, peer), device_id_type=MESH,
        ))
    mine = pl.ds(node * CAP, CAP)
    copies += [
        pltpu.make_async_copy(terms_ref.at[mine], back_ref.at[mine], self_sem.at[0]),
        pltpu.make_async_copy(
            rows_ref.at[band(feat, depth)], activ_ref.at[:, band(feat, width)], self_sem.at[1]
        ),
    ]
    for copy in parts + copies:
        copy.start()

    for copy in parts:
        copy.wait()
    total = part_ref[feat].astype(jnp.float32)
    for i in range(feats - 1):
        total += feat_in[i].astype(jnp.float32)
    partial[...] = total.astype(jnp.bfloat16)
    slices = []
    for off in range(1, shards):
        peer = lax.rem(node + off, shards)
        slices.append(pltpu.make_async_remote_copy(
            src_ref=partial.at[peer], dst_ref=node_in.at[off - 1],
            send_sem=q_send.at[off - 1], recv_sem=q_recv.at[off - 1],
            device_id=(peer, feat), device_id_type=MESH,
        ))
    for copy in slices:
        copy.start()
    for copy in slices:
        copy.wait()
    total = partial[node].astype(jnp.float32)
    for i in range(shards - 1):
        total += node_in[i].astype(jnp.float32)
    reduced[...] = total.astype(jnp.bfloat16)
    spreads = []
    for off in range(1, shards):
        peer = lax.rem(node + off, shards)
        spreads.append(pltpu.make_async_remote_copy(
            src_ref=reduced, dst_ref=gathered.at[node],
            send_sem=r_send.at[off - 1], recv_sem=r_recv.at[off - 1],
            device_id=(peer, feat), device_id_type=MESH,
        ))
    for copy in spreads:
        copy.start()
    gathered[node] = reduced[...]
    for copy in spreads:
        copy.wait()
    grad_ref[...] = gathered[...].astype(jnp.float32) * scale
    for copy in copies:
        copy.wait()


def merge_kernel(shards, blocks, asked_ref, own_ref, back_ref, out_ref, acc):
    node = lax.axis_index("node")
    acc[...] = own_ref[...]
    for off in range(1, shards):
        peer = lax.rem(node + off, shards)

        @pl.loop(0, CAP)
        def _(k):
            acc[asked_ref[peer, k]] += back_ref[peer * CAP + k].astype(jnp.float32)

    for b in range(blocks):
        out_ref[:, b * LANES : (b + 1) * LANES] = acc[b].astype(jnp.bfloat16)


def silu_slope(value):
    sig = jax.nn.sigmoid(value)
    return sig * (1.0 + value * (1.0 - sig))


def per_device(shards, feats, x_feat, weight, out_grad, tile_rows, tile_cols, tile_masks):
    depth, local_rows = x_feat.shape
    blocks = local_rows // LANES
    tiles = tile_cols.shape[0]
    hidden = weight.shape[1]
    features = depth * feats
    per_feat = local_rows // feats
    slots = blocks + shards * CAP
    bf16, f32, i32 = jnp.bfloat16, jnp.float32, jnp.int32
    shape = jax.ShapeDtypeStruct
    dma = pltpu.SemaphoreType.DMA
    steps = tiles // GROUP

    need, slot = pl.pallas_call(
        functools.partial(plan_kernel, shards, blocks, tiles),
        out_shape=(shape((shards, LANES), i32), shape((tiles,), i32)),
        in_specs=[spec(SMEM)],
        out_specs=(spec(SMEM), spec(SMEM)),
        scratch_shapes=[SMEM((blocks * shards,), i32), SMEM((shards,), i32)],
    )(tile_cols)

    asked = pl.pallas_call(
        functools.partial(ask_kernel, shards),
        out_shape=shape((shards, 1, LANES), i32),
        in_specs=[spec(VMEM)],
        out_specs=spec(VMEM),
        scratch_shapes=[dma((shards - 1,)), dma((shards - 1,)), dma(())],
        compiler_params=params(16, collective_id=2, has_side_effects=True),
    )(need.reshape(shards, 1, LANES)).reshape(shards, LANES)

    outbox = pl.pallas_call(
        functools.partial(pick_kernel, shards),
        out_shape=shape((shards * CAP, depth, LANES), bf16),
        in_specs=[spec(SMEM), spec(VMEM)],
        out_specs=spec(VMEM),
        compiler_params=params(24),
    )(asked, x_feat)

    source, cotangent_rows, full_weight = pl.pallas_call(
        functools.partial(fetch_kernel, shards, feats, blocks),
        out_shape=(
            shape((slots, depth, LANES), bf16),
            shape((features, per_feat), bf16),
            shape((features, hidden), bf16),
        ),
        in_specs=[spec(ANY)] * 4,
        out_specs=(spec(ANY),) * 3,
        scratch_shapes=[
            dma((shards - 1,)), dma((shards - 1,)), dma((blocks,)),
            dma((feats - 1,)), dma((feats - 1,)), dma((feats - 1,)), dma((feats - 1,)),
            dma((3,)),
        ],
        compiler_params=params(24, collective_id=0, has_side_effects=True),
    )(outbox, x_feat, out_grad, weight)

    whole3 = lambda i, *_: (0, 0, 0)
    whole2 = lambda i, *_: (0, 0)
    by_tile = lambda i, *_: (i, 0, 0)
    aggregated, degree, edges = pl.pallas_call(
        functools.partial(gather_kernel, steps, blocks),
        grid_spec=pltpu.PrefetchScalarGridSpec(
            num_scalar_prefetch=2,
            grid=(steps,),
            in_specs=[
                pl.BlockSpec((slots, depth, LANES), whole3),
                pl.BlockSpec((GROUP, LANES, LANES), by_tile),
            ],
            out_specs=(
                pl.BlockSpec((depth, local_rows), whole2),
                pl.BlockSpec((blocks, 1, LANES), whole3),
                pl.BlockSpec((GROUP, LANES, LANES), by_tile),
            ),
            scratch_shapes=[VMEM((blocks, depth + 16, LANES), f32)],
        ),
        out_shape=(
            shape((depth, local_rows), bf16),
            shape((blocks, 1, LANES), f32),
            shape((tiles, LANES, LANES), bf16),
        ),
        compiler_params=params(40),
    )(tile_rows, slot, source, tile_masks)

    def swap(array, to_columns, number):
        wide = (depth, local_rows) if to_columns else (features, per_feat)
        return pl.pallas_call(
            functools.partial(swap_kernel, feats, to_columns),
            out_shape=shape(wide, bf16),
            in_specs=[spec(ANY)],
            out_specs=spec(ANY),
            scratch_shapes=[dma((feats - 1,)), dma((feats - 1,)), dma(())],
            compiler_params=params(24, collective_id=number, has_side_effects=True),
        )(array)

    node_rows = swap(aggregated, False, 3)
    row_preact = lax.dot_general(
        full_weight, node_rows, (((0,), (0,)), ((), ())), preferred_element_type=f32
    )
    row_activ = jax.nn.silu(row_preact).astype(bf16)
    grad_rows = (cotangent_rows.astype(f32) * silu_slope(row_preact)).astype(bf16)
    row_hidden = jnp.dot(full_weight, grad_rows, preferred_element_type=f32).astype(bf16)
    full_part = lax.dot_general(
        node_rows, grad_rows, (((1,), (1,)), ((), ())), preferred_element_type=f32
    )
    slice_rows = depth // shards
    full_part = full_part.astype(bf16).reshape(feats, shards, slice_rows, hidden)
    hidden_grad = swap(row_hidden, True, 4)

    own, terms = pl.pallas_call(
        functools.partial(spread_kernel, steps, blocks),
        grid_spec=pltpu.PrefetchScalarGridSpec(
            num_scalar_prefetch=2,
            grid=(steps,),
            in_specs=[
                pl.BlockSpec((depth, local_rows), whole2),
                pl.BlockSpec((blocks, 1, LANES), whole3),
                pl.BlockSpec((GROUP, LANES, LANES), by_tile),
            ],
            out_specs=(
                pl.BlockSpec((blocks, depth, LANES), whole3),
                pl.BlockSpec((shards * CAP, depth, LANES), whole3),
            ),
            scratch_shapes=[
                VMEM((slots, depth, LANES), f32),
                VMEM((blocks, depth, LANES), bf16),
            ],
        ),
        out_shape=(
            shape((blocks, depth, LANES), f32),
            shape((shards * CAP, depth, LANES), bf16),
        ),
        compiler_params=params(40),
    )(tile_rows, slot, hidden_grad, degree, edges)

    piece = (slice_rows, hidden)
    back, activ, weight_grad = pl.pallas_call(
        functools.partial(return_kernel, shards, feats, (local_rows * shards) ** (-0.5)),
        out_shape=(
            shape((shards * CAP, depth, LANES), bf16),
            shape((depth, local_rows), bf16),
            shape((shards, *piece), f32),
        ),
        in_specs=[spec(ANY), spec(ANY), spec(VMEM)],
        out_specs=(spec(ANY), spec(ANY), spec(VMEM)),
        scratch_shapes=[
            VMEM((feats - 1, shards, *piece), bf16), VMEM((shards, *piece), bf16),
            VMEM((shards - 1, *piece), bf16), VMEM(piece, bf16), VMEM((shards, *piece), bf16),
            dma((shards - 1,)), dma((shards - 1,)), dma((feats - 1,)), dma((feats - 1,)), dma((2,)),
            dma((feats - 1,)), dma((feats - 1,)), dma((shards - 1,)), dma((shards - 1,)),
            dma((shards - 1,)), dma((shards - 1,)),
        ],
        compiler_params=params(24, collective_id=1, has_side_effects=True),
    )(terms, row_activ, full_part)
    weight_grad = weight_grad.reshape(depth, hidden)

    x_grad = pl.pallas_call(
        functools.partial(merge_kernel, shards, blocks),
        out_shape=shape((depth, local_rows), bf16),
        in_specs=[spec(SMEM), spec(VMEM), spec(VMEM)],
        out_specs=spec(VMEM),
        scratch_shapes=[VMEM((blocks, depth, LANES), f32)],
        compiler_params=params(32),
    )(asked, own, back)
    return (activ, x_grad, weight_grad)


def solution(mesh):
    placed = (
        P("feat", "node"),
        P("feat", None),
        P("feat", "node"),
        P("node"),
        P("node"),
        P("node", None, None),
    )
    return jax.shard_map(
        functools.partial(per_device, mesh.shape["node"], mesh.shape["feat"]),
        mesh=mesh,
        in_specs=placed,
        out_specs=(P("feat", "node"), P("feat", "node"), P("feat", None)),
        check_vma=False,
    )
```

```python
import functools

import jax
import jax.numpy as jnp
from jax import lax
from jax.experimental import pallas as pl
from jax.experimental.pallas import tpu as pltpu
from jax.sharding import PartitionSpec as P

CAP = 8
GROUP = 8
LANES = 128
MESH = pl.DeviceIdType.MESH
VMEM = pltpu.VMEM
SMEM = pltpu.SMEM
ANY = pl.ANY


def spec(space):
    return pl.BlockSpec(memory_space=space)


def params(limit_mib, **more):
    return pltpu.CompilerParams(vmem_limit_bytes=limit_mib << 20, **more)


def barrier(shards, feats):
    node, feat = lax.axis_index("node"), lax.axis_index("feat")
    sem = pltpu.get_barrier_semaphore()
    for off in range(1, shards):
        pl.semaphore_signal(
            sem, inc=1, device_id=(lax.rem(node + off, shards), feat), device_id_type=MESH
        )
    for off in range(1, feats):
        pl.semaphore_signal(
            sem, inc=1, device_id=(node, lax.rem(feat + off, feats)), device_id_type=MESH
        )
    pl.semaphore_wait(sem, max(shards - 1, 0) + max(feats - 1, 0))


def ask_kernel(
    shards, blocks, cols_ref, asked_ref, slot_ref, need, send_sem, recv_sem, self_sem
):
    node, feat = lax.axis_index("node"), lax.axis_index("feat")
    barrier(shards, 0)
    columns, tiles = shards * blocks, cols_ref.shape[1]
    f32, bf16 = jnp.float32, jnp.bfloat16

    def iota(dims, axis):
        return lax.broadcasted_iota(jnp.int32, dims, axis)

    def contract_columns(left, right):
        return lax.dot_general(left, right, (((0,), (0,)), ((), ())), preferred_element_type=f32)

    hits = (iota((columns, tiles), 0) == cols_ref[...]).astype(f32)
    present = jnp.minimum(jnp.sum(hits, axis=1, keepdims=True), 1.0)
    present = jnp.broadcast_to(present, (columns, LANES))
    below, above = iota((columns, columns), 0), iota((columns, columns), 1)
    earlier = ((below < above) & (below // blocks == above // blocks)).astype(f32).astype(bf16)
    order = contract_columns(earlier, present.astype(bf16))
    column, lane = iota((columns, LANES), 0), iota((columns, LANES), 1)
    shard = column // blocks
    local = (column - shard * blocks).astype(f32)
    chosen = jnp.where(order == lane.astype(f32), present * local, 0.0).astype(bf16)
    of_shard = (iota((columns, LANES), 0) // blocks == iota((columns, LANES), 1)).astype(f32)
    lists = contract_columns(of_shard.astype(bf16), chosen).astype(jnp.int32)
    for s in range(shards):
        need[s] = lists[s : s + 1]
    copies = []
    for off in range(1, shards):
        peer = lax.rem(node + off, shards)
        copy = pltpu.make_async_remote_copy(
            src_ref=need.at[peer], dst_ref=asked_ref.at[node],
            send_sem=send_sem.at[off - 1], recv_sem=recv_sem.at[off - 1],
            device_id=(peer, feat), device_id_type=MESH,
        )
        copy.start()
        copies.append(copy)
    own = pltpu.make_async_copy(need.at[node], asked_ref.at[node], self_sem)
    own.start()
    away = order + (shard * CAP + blocks).astype(f32)
    place = jnp.where(shard == node, local, jnp.minimum(away, 255.0)).astype(bf16)
    slot_ref[...] = contract_columns(place, hits.astype(bf16))[:1].astype(jnp.int32)
    own.wait()
    for copy in copies:
        copy.wait()


def pick_kernel(shards, asked_ref, x_ref, outbox_ref):
    for s in range(shards):

        @pl.loop(0, CAP)
        def _(k):
            columns = pl.ds(pl.multiple_of(asked_ref[s, k] * LANES, LANES), LANES)
            outbox_ref[s * CAP + k] = x_ref[:, columns]


def fetch_kernel(
    shards, feats, blocks, outbox_ref, x_ref, grad_ref, weight_ref, mask_ref, source_ref,
    cot_ref, full_ref, edge_ref, turned_ref, masks, edges, turned, mask_sem, x_send, x_recv, own_sem, cot_send, cot_recv, w_send, w_recv, self_sem,
):
    node, feat = lax.axis_index("node"), lax.axis_index("feat")
    depth = x_ref.shape[0]
    per_feat = cot_ref.shape[1]
    barrier(shards, feats)
    mine = pl.ds(node * CAP, CAP)
    landing = pl.ds(blocks + node * CAP, CAP)

    copies = []
    for off in range(1, shards):
        peer = lax.rem(node + off, shards)
        copies.append(pltpu.make_async_remote_copy(
            src_ref=outbox_ref.at[pl.ds(peer * CAP, CAP)], dst_ref=source_ref.at[landing],
            send_sem=x_send.at[off - 1], recv_sem=x_recv.at[off - 1],
            device_id=(peer, feat), device_id_type=MESH,
        ))
    rows = pl.ds(pl.multiple_of(feat * depth, depth), depth)
    for off in range(1, feats):
        peer = lax.rem(feat + off, feats)
        columns = pl.ds(pl.multiple_of(peer * per_feat, per_feat), per_feat)
        for src, dst, sent, got in (
            (weight_ref, full_ref.at[rows], w_send, w_recv),
            (grad_ref.at[:, columns], cot_ref.at[rows], cot_send, cot_recv),
        ):
            copies.append(pltpu.make_async_remote_copy(
                src_ref=src, dst_ref=dst, send_sem=sent.at[off - 1], recv_sem=got.at[off - 1],
                device_id=(node, peer), device_id_type=MESH,
            ))
    own = pl.ds(pl.multiple_of(feat * per_feat, per_feat), per_feat)
    copies += [
        pltpu.make_async_copy(weight_ref, full_ref.at[rows], self_sem.at[0]),
        pltpu.make_async_copy(grad_ref.at[:, own], cot_ref.at[rows], self_sem.at[1]),
        pltpu.make_async_copy(outbox_ref.at[mine], source_ref.at[landing], self_sem.at[2]),
    ]
    for b in range(blocks):
        copies.append(pltpu.make_async_copy(
            x_ref.at[:, pl.ds(b * LANES, LANES)], source_ref.at[b], own_sem.at[b]
        ))
    load = pltpu.make_async_copy(mask_ref, masks, mask_sem.at[0])
    load.start()
    for copy in copies:
        copy.start()
    load.wait()

    @pl.loop(0, masks.shape[0] // GROUP)
    def _(i):
        for g in range(GROUP):
            value = masks[i * GROUP + g].astype(jnp.float32)
            edges[i * GROUP + g] = value.astype(jnp.bfloat16)
            turned[i * GROUP + g] = value.T.astype(jnp.bfloat16)

    stores = [
        pltpu.make_async_copy(edges, edge_ref, mask_sem.at[1]),
        pltpu.make_async_copy(turned, turned_ref, mask_sem.at[2]),
    ]
    for copy in stores:
        copy.start()
    for copy in stores + copies:
        copy.wait()


def gather_kernel(steps, blocks, rows_ref, slot_ref, source_ref, turned_ref, agg_ref, deg_ref, acc):
    step = pl.program_id(0)
    depth = source_ref.shape[1]
    ones = jnp.ones((16, LANES), jnp.bfloat16)

    def term(g):
        t = step * GROUP + g
        source = jnp.concatenate([source_ref[slot_ref[t]], ones], axis=0)
        return rows_ref[t], jnp.dot(source, turned_ref[g], preferred_element_type=jnp.float32)

    @pl.when(step < blocks // GROUP)
    def _():
        for g in range(GROUP):
            row, value = term(g)
            acc[row] = value

    @pl.when(step >= blocks // GROUP)
    def _():
        for g in range(0, GROUP, 2):
            row0, value0 = term(g)
            row1, value1 = term(g + 1)
            acc[row0] += value0
            acc[row1] += value1

    @pl.when(step == steps - 1)
    def _():
        for b in range(blocks):
            degree = 1.0 + acc[b, depth : depth + 1, :]
            mixed = source_ref[b].astype(jnp.float32) + acc[b, :depth, :]
            agg_ref[:, b * LANES : (b + 1) * LANES] = (mixed / degree).astype(jnp.bfloat16)
            deg_ref[b] = degree


def spread_kernel(steps, blocks, rows_ref, slot_ref, hidden_ref, deg_ref, edge_ref, own_ref, terms_ref, acc, scaled):
    step = pl.program_id(0)

    @pl.when(step == 0)
    def _():
        for b in range(blocks):
            value = hidden_ref[:, b * LANES : (b + 1) * LANES].astype(jnp.float32) / deg_ref[b]
            value = value.astype(jnp.bfloat16)
            scaled[b] = value
            acc[b] = value.astype(jnp.float32)
        acc[blocks:] = jnp.zeros_like(acc[blocks:])

    def term(g):
        t = step * GROUP + g
        return slot_ref[t], jnp.dot(
            scaled[rows_ref[t]], edge_ref[g], preferred_element_type=jnp.float32
        )

    for g in range(0, GROUP, 2):
        slot0, value0 = term(g)
        slot1, value1 = term(g + 1)
        acc[slot0] += value0
        acc[slot1] += value1

    @pl.when(step == steps - 1)
    def _():
        own_ref[...] = acc[:blocks]
        terms_ref[...] = acc[blocks:].astype(jnp.bfloat16)


def band(index, size):
    return pl.ds(pl.multiple_of(index * size, size), size)


def swap_kernel(feats, to_columns, src_ref, dst_ref, send_sem, recv_sem, self_sem):
    node, feat = lax.axis_index("node"), lax.axis_index("feat")
    barrier(0, feats)
    depth = min(src_ref.shape[0], dst_ref.shape[0])
    width = min(src_ref.shape[1], dst_ref.shape[1])

    def ends(peer):
        if to_columns:
            return src_ref.at[band(peer, depth)], dst_ref.at[:, band(feat, width)]
        return src_ref.at[:, band(peer, width)], dst_ref.at[band(feat, depth)]

    copies = []
    for off in range(1, feats):
        peer = lax.rem(feat + off, feats)
        src, dst = ends(peer)
        copies.append(pltpu.make_async_remote_copy(
            src_ref=src, dst_ref=dst, send_sem=send_sem.at[off - 1],
            recv_sem=recv_sem.at[off - 1], device_id=(node, peer), device_id_type=MESH,
        ))
    src, dst = ends(feat)
    copies.append(pltpu.make_async_copy(src, dst, self_sem))
    for copy in copies:
        copy.start()
    for copy in copies:
        copy.wait()


def return_kernel(
    shards, feats, scale, terms_ref, rows_ref, part_ref, back_ref, activ_ref, grad_ref,
    feat_in, partial, node_in, reduced, gathered, z_send, z_recv, a_send, a_recv, self_sem,
    p_send, p_recv, q_send, q_recv, r_send, r_recv,
):
    node, feat = lax.axis_index("node"), lax.axis_index("feat")
    depth = activ_ref.shape[0]
    width = rows_ref.shape[1]
    barrier(shards, feats)

    parts = []
    for off in range(1, feats):
        peer = lax.rem(feat + off, feats)
        parts.append(pltpu.make_async_remote_copy(
            src_ref=part_ref.at[peer], dst_ref=feat_in.at[off - 1],
            send_sem=p_send.at[off - 1], recv_sem=p_recv.at[off - 1],
            device_id=(node, peer), device_id_type=MESH,
        ))
    copies = []
    for off in range(1, shards):
        peer = lax.rem(node + off, shards)
        copies.append(pltpu.make_async_remote_copy(
            src_ref=terms_ref.at[pl.ds(peer * CAP, CAP)],
            dst_ref=back_ref.at[pl.ds(node * CAP, CAP)],
            send_sem=z_send.at[off - 1], recv_sem=z_recv.at[off - 1],
            device_id=(peer, feat), device_id_type=MESH,
        ))
    for off in range(1, feats):
        peer = lax.rem(feat + off, feats)
        copies.append(pltpu.make_async_remote_copy(
            src_ref=rows_ref.at[band(peer, depth)], dst_ref=activ_ref.at[:, band(feat, width)],
            send_sem=a_send.at[off - 1], recv_sem=a_recv.at[off - 1],
            device_id=(node, peer), device_id_type=MESH,
        ))
    mine = pl.ds(node * CAP, CAP)
    copies += [
        pltpu.make_async_copy(terms_ref.at[mine], back_ref.at[mine], self_sem.at[0]),
        pltpu.make_async_copy(
            rows_ref.at[band(feat, depth)], activ_ref.at[:, band(feat, width)], self_sem.at[1]
        ),
    ]
    for copy in parts + copies:
        copy.start()

    for copy in parts:
        copy.wait()
    total = part_ref[feat].astype(jnp.float32)
    for i in range(feats - 1):
        total += feat_in[i].astype(jnp.float32)
    partial[...] = total.astype(jnp.bfloat16)
    slices = []
    for off in range(1, shards):
        peer = lax.rem(node + off, shards)
        slices.append(pltpu.make_async_remote_copy(
            src_ref=partial.at[peer], dst_ref=node_in.at[off - 1],
            send_sem=q_send.at[off - 1], recv_sem=q_recv.at[off - 1],
            device_id=(peer, feat), device_id_type=MESH,
        ))
    for copy in slices:
        copy.start()
    for copy in slices:
        copy.wait()
    total = partial[node].astype(jnp.float32)
    for i in range(shards - 1):
        total += node_in[i].astype(jnp.float32)
    reduced[...] = total.astype(jnp.bfloat16)
    spreads = []
    for off in range(1, shards):
        peer = lax.rem(node + off, shards)
        spreads.append(pltpu.make_async_remote_copy(
            src_ref=reduced, dst_ref=gathered.at[node],
            send_sem=r_send.at[off - 1], recv_sem=r_recv.at[off - 1],
            device_id=(peer, feat), device_id_type=MESH,
        ))
    for copy in spreads:
        copy.start()
    gathered[node] = reduced[...]
    for copy in spreads:
        copy.wait()
    grad_ref[...] = gathered[...].astype(jnp.float32) * scale
    for copy in copies:
        copy.wait()


def merge_kernel(shards, blocks, asked_ref, own_ref, back_ref, out_ref, acc):
    node = lax.axis_index("node")
    acc[...] = own_ref[...]
    for off in range(1, shards):
        peer = lax.rem(node + off, shards)

        @pl.loop(0, CAP)
        def _(k):
            acc[asked_ref[peer, k]] += back_ref[peer * CAP + k].astype(jnp.float32)

    for b in range(blocks):
        out_ref[:, b * LANES : (b + 1) * LANES] = acc[b].astype(jnp.bfloat16)


def silu_slope(value):
    sig = jax.nn.sigmoid(value)
    return sig * (1.0 + value * (1.0 - sig))


def per_device(shards, feats, x_feat, weight, out_grad, tile_rows, tile_cols, tile_masks):
    depth, local_rows = x_feat.shape
    blocks = local_rows // LANES
    tiles = tile_cols.shape[0]
    hidden = weight.shape[1]
    features = depth * feats
    per_feat = local_rows // feats
    slots = blocks + shards * CAP
    bf16, f32, i32 = jnp.bfloat16, jnp.float32, jnp.int32
    shape = jax.ShapeDtypeStruct
    dma = pltpu.SemaphoreType.DMA
    steps = tiles // GROUP

    asked, slot = pl.pallas_call(
        functools.partial(ask_kernel, shards, blocks),
        out_shape=(shape((shards, 1, LANES), i32), shape((1, tiles), i32)),
        in_specs=[spec(VMEM)],
        out_specs=(spec(VMEM), spec(VMEM)),
        scratch_shapes=[
            VMEM((shards, 1, LANES), i32), dma((shards - 1,)), dma((shards - 1,)), dma(()),
        ],
        compiler_params=params(16, collective_id=2, has_side_effects=True),
    )(tile_cols.reshape(1, tiles))
    asked, slot = asked.reshape(shards, LANES), slot.reshape(tiles)

    outbox = pl.pallas_call(
        functools.partial(pick_kernel, shards),
        out_shape=shape((shards * CAP, depth, LANES), bf16),
        in_specs=[spec(SMEM), spec(VMEM)],
        out_specs=spec(VMEM),
        compiler_params=params(24),
    )(asked, x_feat)

    source, cotangent_rows, full_weight, edges, turned = pl.pallas_call(
        functools.partial(fetch_kernel, shards, feats, blocks),
        out_shape=(
            shape((slots, depth, LANES), bf16),
            shape((features, per_feat), bf16),
            shape((features, hidden), bf16),
            shape((tiles, LANES, LANES), bf16),
            shape((tiles, LANES, LANES), bf16),
        ),
        in_specs=[spec(ANY)] * 5,
        out_specs=(spec(ANY),) * 5,
        scratch_shapes=[
            VMEM((tiles, LANES, LANES), i32),
            VMEM((tiles, LANES, LANES), bf16), VMEM((tiles, LANES, LANES), bf16), dma((3,)),
            dma((shards - 1,)), dma((shards - 1,)), dma((blocks,)),
            dma((feats - 1,)), dma((feats - 1,)), dma((feats - 1,)), dma((feats - 1,)),
            dma((3,)),
        ],
        compiler_params=params(40, collective_id=0, has_side_effects=True),
    )(outbox, x_feat, out_grad, weight, tile_masks)

    whole3 = lambda i, *_: (0, 0, 0)
    whole2 = lambda i, *_: (0, 0)
    by_tile = lambda i, *_: (i, 0, 0)
    aggregated, degree = pl.pallas_call(
        functools.partial(gather_kernel, steps, blocks),
        grid_spec=pltpu.PrefetchScalarGridSpec(
            num_scalar_prefetch=2,
            grid=(steps,),
            in_specs=[
                pl.BlockSpec((slots, depth, LANES), whole3),
                pl.BlockSpec((GROUP, LANES, LANES), by_tile),
            ],
            out_specs=(
                pl.BlockSpec((depth, local_rows), whole2),
                pl.BlockSpec((blocks, 1, LANES), whole3),
            ),
            scratch_shapes=[VMEM((blocks, depth + 16, LANES), f32)],
        ),
        out_shape=(
            shape((depth, local_rows), bf16),
            shape((blocks, 1, LANES), f32),
        ),
        compiler_params=params(40),
    )(tile_rows, slot, source, turned)

    def swap(array, to_columns, number):
        wide = (depth, local_rows) if to_columns else (features, per_feat)
        return pl.pallas_call(
            functools.partial(swap_kernel, feats, to_columns),
            out_shape=shape(wide, bf16),
            in_specs=[spec(ANY)],
            out_specs=spec(ANY),
            scratch_shapes=[dma((feats - 1,)), dma((feats - 1,)), dma(())],
            compiler_params=params(24, collective_id=number, has_side_effects=True),
        )(array)

    node_rows = swap(aggregated, False, 3)
    row_preact = lax.dot_general(
        full_weight, node_rows, (((0,), (0,)), ((), ())), preferred_element_type=f32
    )
    row_activ = jax.nn.silu(row_preact).astype(bf16)
    grad_rows = (cotangent_rows.astype(f32) * silu_slope(row_preact)).astype(bf16)
    row_hidden = jnp.dot(full_weight, grad_rows, preferred_element_type=f32).astype(bf16)
    full_part = lax.dot_general(
        node_rows, grad_rows, (((1,), (1,)), ((), ())), preferred_element_type=f32
    )
    slice_rows = depth // shards
    full_part = full_part.astype(bf16).reshape(feats, shards, slice_rows, hidden)
    hidden_grad = swap(row_hidden, True, 4)

    own, terms = pl.pallas_call(
        functools.partial(spread_kernel, steps, blocks),
        grid_spec=pltpu.PrefetchScalarGridSpec(
            num_scalar_prefetch=2,
            grid=(steps,),
            in_specs=[
                pl.BlockSpec((depth, local_rows), whole2),
                pl.BlockSpec((blocks, 1, LANES), whole3),
                pl.BlockSpec((GROUP, LANES, LANES), by_tile),
            ],
            out_specs=(
                pl.BlockSpec((blocks, depth, LANES), whole3),
                pl.BlockSpec((shards * CAP, depth, LANES), whole3),
            ),
            scratch_shapes=[
                VMEM((slots, depth, LANES), f32),
                VMEM((blocks, depth, LANES), bf16),
            ],
        ),
        out_shape=(
            shape((blocks, depth, LANES), f32),
            shape((shards * CAP, depth, LANES), bf16),
        ),
        compiler_params=params(40),
    )(tile_rows, slot, hidden_grad, degree, edges)

    piece = (slice_rows, hidden)
    back, activ, weight_grad = pl.pallas_call(
        functools.partial(return_kernel, shards, feats, (local_rows * shards) ** (-0.5)),
        out_shape=(
            shape((shards * CAP, depth, LANES), bf16),
            shape((depth, local_rows), bf16),
            shape((shards, *piece), f32),
        ),
        in_specs=[spec(ANY), spec(ANY), spec(VMEM)],
        out_specs=(spec(ANY), spec(ANY), spec(VMEM)),
        scratch_shapes=[
            VMEM((feats - 1, shards, *piece), bf16), VMEM((shards, *piece), bf16),
            VMEM((shards - 1, *piece), bf16), VMEM(piece, bf16), VMEM((shards, *piece), bf16),
            dma((shards - 1,)), dma((shards - 1,)), dma((feats - 1,)), dma((feats - 1,)), dma((2,)),
            dma((feats - 1,)), dma((feats - 1,)), dma((shards - 1,)), dma((shards - 1,)),
            dma((shards - 1,)), dma((shards - 1,)),
        ],
        compiler_params=params(24, collective_id=1, has_side_effects=True),
    )(terms, row_activ, full_part)
    weight_grad = weight_grad.reshape(depth, hidden)

    x_grad = pl.pallas_call(
        functools.partial(merge_kernel, shards, blocks),
        out_shape=shape((depth, local_rows), bf16),
        in_specs=[spec(SMEM), spec(VMEM), spec(VMEM)],
        out_specs=spec(VMEM),
        scratch_shapes=[VMEM((blocks, depth, LANES), f32)],
        compiler_params=params(32),
    )(asked, own, back)
    return (activ, x_grad, weight_grad)


def solution(mesh):
    placed = (
        P("feat", "node"),
        P("feat", None),
        P("feat", "node"),
        P("node"),
        P("node"),
        P("node", None, None),
    )
    return jax.shard_map(
        functools.partial(per_device, mesh.shape["node"], mesh.shape["feat"]),
        mesh=mesh,
        in_specs=placed,
        out_specs=(P("feat", "node"), P("feat", "node"), P("feat", None)),
        check_vma=False,
    )
```

```python
import functools

import jax
import jax.numpy as jnp
from jax import lax
from jax.experimental import pallas as pl
from jax.experimental.pallas import tpu as pltpu
from jax.sharding import PartitionSpec as P

CAP = 8
GROUP = 8
LANES = 128
MESH = pl.DeviceIdType.MESH
VMEM = pltpu.VMEM
SMEM = pltpu.SMEM
ANY = pl.ANY


def spec(space):
    return pl.BlockSpec(memory_space=space)


def params(limit_mib, **more):
    return pltpu.CompilerParams(vmem_limit_bytes=limit_mib << 20, **more)


def barrier(shards, feats):
    node, feat = lax.axis_index("node"), lax.axis_index("feat")
    sem = pltpu.get_barrier_semaphore()
    for off in range(1, shards):
        pl.semaphore_signal(
            sem, inc=1, device_id=(lax.rem(node + off, shards), feat), device_id_type=MESH
        )
    for off in range(1, feats):
        pl.semaphore_signal(
            sem, inc=1, device_id=(node, lax.rem(feat + off, feats)), device_id_type=MESH
        )
    pl.semaphore_wait(sem, max(shards - 1, 0) + max(feats - 1, 0))


def ask_kernel(
    shards, blocks, cols_ref, asked_ref, slot_ref, need, send_sem, recv_sem, self_sem
):
    node, feat = lax.axis_index("node"), lax.axis_index("feat")
    barrier(shards, 0)
    columns, tiles = shards * blocks, cols_ref.shape[1]
    f32, bf16 = jnp.float32, jnp.bfloat16

    def iota(dims, axis):
        return lax.broadcasted_iota(jnp.int32, dims, axis)

    def contract_columns(left, right):
        return lax.dot_general(left, right, (((0,), (0,)), ((), ())), preferred_element_type=f32)

    hits = (iota((columns, tiles), 0) == cols_ref[...]).astype(f32)
    present = jnp.minimum(jnp.sum(hits, axis=1, keepdims=True), 1.0)
    present = jnp.broadcast_to(present, (columns, LANES))
    below, above = iota((columns, columns), 0), iota((columns, columns), 1)
    earlier = ((below < above) & (below // blocks == above // blocks)).astype(f32).astype(bf16)
    order = contract_columns(earlier, present.astype(bf16))
    column, lane = iota((columns, LANES), 0), iota((columns, LANES), 1)
    shard = column // blocks
    local = (column - shard * blocks).astype(f32)
    chosen = jnp.where(order == lane.astype(f32), present * local, 0.0).astype(bf16)
    of_shard = (iota((columns, LANES), 0) // blocks == iota((columns, LANES), 1)).astype(f32)
    lists = contract_columns(of_shard.astype(bf16), chosen).astype(jnp.int32)
    for s in range(shards):
        need[s] = lists[s : s + 1]
    copies = []
    for off in range(1, shards):
        peer = lax.rem(node + off, shards)
        copy = pltpu.make_async_remote_copy(
            src_ref=need.at[peer], dst_ref=asked_ref.at[node],
            send_sem=send_sem.at[off - 1], recv_sem=recv_sem.at[off - 1],
            device_id=(peer, feat), device_id_type=MESH,
        )
        copy.start()
        copies.append(copy)
    own = pltpu.make_async_copy(need.at[node], asked_ref.at[node], self_sem)
    own.start()
    away = order + (shard * CAP + blocks).astype(f32)
    place = jnp.where(shard == node, local, jnp.minimum(away, 255.0)).astype(bf16)
    slot_ref[...] = contract_columns(place, hits.astype(bf16))[:1].astype(jnp.int32)
    own.wait()
    for copy in copies:
        copy.wait()


def pick_kernel(shards, asked_ref, x_ref, outbox_ref):
    for s in range(shards):

        @pl.loop(0, CAP)
        def _(k):
            columns = pl.ds(pl.multiple_of(asked_ref[s, k] * LANES, LANES), LANES)
            outbox_ref[s * CAP + k] = x_ref[:, columns]


def fetch_kernel(
    shards, feats, blocks, outbox_ref, x_ref, grad_ref, weight_ref, mask_ref, source_ref,
    cot_ref, full_ref, edge_ref, turned_ref, masks, edges, turned, mask_sem, x_send, x_recv, own_sem, cot_send, cot_recv, w_send, w_recv, self_sem,
):
    node, feat = lax.axis_index("node"), lax.axis_index("feat")
    depth = x_ref.shape[0]
    per_feat = cot_ref.shape[1]
    barrier(shards, feats)
    mine = pl.ds(node * CAP, CAP)
    landing = pl.ds(blocks + node * CAP, CAP)

    copies = []
    for off in range(1, shards):
        peer = lax.rem(node + off, shards)
        copies.append(pltpu.make_async_remote_copy(
            src_ref=outbox_ref.at[pl.ds(peer * CAP, CAP)], dst_ref=source_ref.at[landing],
            send_sem=x_send.at[off - 1], recv_sem=x_recv.at[off - 1],
            device_id=(peer, feat), device_id_type=MESH,
        ))
    rows = pl.ds(pl.multiple_of(feat * depth, depth), depth)
    for off in range(1, feats):
        peer = lax.rem(feat + off, feats)
        columns = pl.ds(pl.multiple_of(peer * per_feat, per_feat), per_feat)
        for src, dst, sent, got in (
            (weight_ref, full_ref.at[rows], w_send, w_recv),
            (grad_ref.at[:, columns], cot_ref.at[rows], cot_send, cot_recv),
        ):
            copies.append(pltpu.make_async_remote_copy(
                src_ref=src, dst_ref=dst, send_sem=sent.at[off - 1], recv_sem=got.at[off - 1],
                device_id=(node, peer), device_id_type=MESH,
            ))
    own = pl.ds(pl.multiple_of(feat * per_feat, per_feat), per_feat)
    copies += [
        pltpu.make_async_copy(weight_ref, full_ref.at[rows], self_sem.at[0]),
        pltpu.make_async_copy(grad_ref.at[:, own], cot_ref.at[rows], self_sem.at[1]),
        pltpu.make_async_copy(outbox_ref.at[mine], source_ref.at[landing], self_sem.at[2]),
    ]
    for b in range(blocks):
        copies.append(pltpu.make_async_copy(
            x_ref.at[:, pl.ds(b * LANES, LANES)], source_ref.at[b], own_sem.at[b]
        ))
    load = pltpu.make_async_copy(mask_ref, masks, mask_sem.at[0])
    load.start()
    for copy in copies:
        copy.start()
    load.wait()

    @pl.loop(0, masks.shape[0] // GROUP)
    def _(i):
        for g in range(GROUP):
            value = masks[i * GROUP + g].astype(jnp.float32)
            edges[i * GROUP + g] = value.astype(jnp.bfloat16)
            turned[i * GROUP + g] = value.T.astype(jnp.bfloat16)

    stores = [
        pltpu.make_async_copy(edges, edge_ref, mask_sem.at[1]),
        pltpu.make_async_copy(turned, turned_ref, mask_sem.at[2]),
    ]
    for copy in stores:
        copy.start()
    for copy in stores + copies:
        copy.wait()


def gather_kernel(steps, blocks, rows_ref, slot_ref, source_ref, turned_ref, agg_ref, deg_ref, acc):
    step = pl.program_id(0)
    depth = source_ref.shape[1]
    ones = jnp.ones((16, LANES), jnp.bfloat16)

    def term(g):
        t = step * GROUP + g
        source = jnp.concatenate([source_ref[slot_ref[t]], ones], axis=0)
        return rows_ref[t], jnp.dot(source, turned_ref[g], preferred_element_type=jnp.float32)

    @pl.when(step < blocks // GROUP)
    def _():
        for g in range(GROUP):
            row, value = term(g)
            acc[row] = value

    @pl.when(step >= blocks // GROUP)
    def _():
        for g in range(0, GROUP, 2):
            row0, value0 = term(g)
            row1, value1 = term(g + 1)
            acc[row0] += value0
            acc[row1] += value1

    @pl.when(step == steps - 1)
    def _():
        for b in range(blocks):
            degree = 1.0 + acc[b, depth : depth + 1, :]
            mixed = source_ref[b].astype(jnp.float32) + acc[b, :depth, :]
            agg_ref[:, b * LANES : (b + 1) * LANES] = (mixed / degree).astype(jnp.bfloat16)
            deg_ref[b] = degree


def spread_kernel(steps, blocks, rows_ref, slot_ref, hidden_ref, deg_ref, edge_ref, own_ref, terms_ref, acc, scaled):
    step = pl.program_id(0)

    @pl.when(step == 0)
    def _():
        for b in range(blocks):
            value = hidden_ref[:, b * LANES : (b + 1) * LANES].astype(jnp.float32) / deg_ref[b]
            value = value.astype(jnp.bfloat16)
            scaled[b] = value
            acc[b] = value.astype(jnp.float32)
        acc[blocks:] = jnp.zeros_like(acc[blocks:])

    def term(g):
        t = step * GROUP + g
        return slot_ref[t], jnp.dot(
            scaled[rows_ref[t]], edge_ref[g], preferred_element_type=jnp.float32
        )

    for g in range(0, GROUP, 2):
        slot0, value0 = term(g)
        slot1, value1 = term(g + 1)
        acc[slot0] += value0
        acc[slot1] += value1

    @pl.when(step == steps - 1)
    def _():
        own_ref[...] = acc[:blocks]
        terms_ref[...] = acc[blocks:].astype(jnp.bfloat16)


def band(index, size):
    return pl.ds(pl.multiple_of(index * size, size), size)


def dense_kernel(
    feats, parts, agg_ref, cot_ref, weight_ref, hidden_ref, activ_ref, part_ref,
    nodes, grads, outgoing, turned, in_send, in_recv, out_send, out_recv, self_sem,
):
    node, feat = lax.axis_index("node"), lax.axis_index("feat")
    depth = agg_ref.shape[0]
    per_feat = nodes.shape[1]
    width = per_feat // parts
    barrier(0, feats)
    arrivals, selfs = [], []
    for c in range(parts):
        here = pl.ds(c * width, width)
        arrivals.append([])
        for off in range(1, feats):
            peer = lax.rem(feat + off, feats)
            columns = pl.ds(pl.multiple_of(peer * per_feat + c * width, width), width)
            arrivals[c].append(pltpu.make_async_remote_copy(
                src_ref=agg_ref.at[:, columns], dst_ref=nodes.at[band(feat, depth), here],
                send_sem=in_send.at[c, off - 1], recv_sem=in_recv.at[c, off - 1],
                device_id=(node, peer), device_id_type=MESH,
            ))
        columns = pl.ds(pl.multiple_of(feat * per_feat + c * width, width), width)
        selfs.append(pltpu.make_async_copy(
            agg_ref.at[:, columns], nodes.at[band(feat, depth), here], self_sem.at[c]
        ))
    for c in range(parts):
        for copy in arrivals[c] + [selfs[c]]:
            copy.start()
    turned[...] = weight_ref[...].astype(jnp.float32).T.astype(jnp.bfloat16)
    returns = []
    for c in range(parts):
        for copy in arrivals[c] + [selfs[c]]:
            copy.wait()

        @pl.loop(0, width // LANES)
        def _(i):
            columns = pl.ds(pl.multiple_of(c * width + i * LANES, LANES), LANES)
            preact = jnp.dot(turned[...], nodes[:, columns], preferred_element_type=jnp.float32)
            sig = jax.nn.sigmoid(preact)
            activ_ref[:, columns] = (preact * sig).astype(jnp.bfloat16)
            slope = sig * (1.0 + preact * (1.0 - sig))
            grad = (cot_ref[:, columns].astype(jnp.float32) * slope).astype(jnp.bfloat16)
            grads[:, columns] = grad
            outgoing[:, columns] = jnp.dot(
                weight_ref[...], grad, preferred_element_type=jnp.float32
            ).astype(jnp.bfloat16)

        here = pl.ds(c * width, width)
        columns = pl.ds(pl.multiple_of(feat * per_feat + c * width, width), width)
        for off in range(1, feats):
            peer = lax.rem(feat + off, feats)
            returns.append(pltpu.make_async_remote_copy(
                src_ref=outgoing.at[band(peer, depth), here], dst_ref=hidden_ref.at[:, columns],
                send_sem=out_send.at[c, off - 1], recv_sem=out_recv.at[c, off - 1],
                device_id=(node, peer), device_id_type=MESH,
            ))
            returns[-1].start()
        returns.append(pltpu.make_async_copy(
            outgoing.at[band(feat, depth), here], hidden_ref.at[:, columns], self_sem.at[parts + c]
        ))
        returns[-1].start()

    @pl.loop(0, part_ref.shape[0] // LANES)
    def _(i):
        rows = pl.ds(pl.multiple_of(i * LANES, LANES), LANES)
        part_ref[rows] = lax.dot_general(
            nodes[rows], grads[...], (((1,), (1,)), ((), ())), preferred_element_type=jnp.float32
        ).astype(jnp.bfloat16)

    for copy in returns:
        copy.wait()


def return_kernel(
    shards, feats, scale, terms_ref, rows_ref, part_ref, back_ref, activ_ref, grad_ref,
    feat_in, partial, node_in, reduced, gathered, z_send, z_recv, a_send, a_recv, self_sem,
    p_send, p_recv, q_send, q_recv, r_send, r_recv,
):
    node, feat = lax.axis_index("node"), lax.axis_index("feat")
    depth = activ_ref.shape[0]
    width = rows_ref.shape[1]
    barrier(shards, feats)

    parts = []
    for off in range(1, feats):
        peer = lax.rem(feat + off, feats)
        parts.append(pltpu.make_async_remote_copy(
            src_ref=part_ref.at[peer], dst_ref=feat_in.at[off - 1],
            send_sem=p_send.at[off - 1], recv_sem=p_recv.at[off - 1],
            device_id=(node, peer), device_id_type=MESH,
        ))
    copies = []
    for off in range(1, shards):
        peer = lax.rem(node + off, shards)
        copies.append(pltpu.make_async_remote_copy(
            src_ref=terms_ref.at[pl.ds(peer * CAP, CAP)],
            dst_ref=back_ref.at[pl.ds(node * CAP, CAP)],
            send_sem=z_send.at[off - 1], recv_sem=z_recv.at[off - 1],
            device_id=(peer, feat), device_id_type=MESH,
        ))
    for off in range(1, feats):
        peer = lax.rem(feat + off, feats)
        copies.append(pltpu.make_async_remote_copy(
            src_ref=rows_ref.at[band(peer, depth)], dst_ref=activ_ref.at[:, band(feat, width)],
            send_sem=a_send.at[off - 1], recv_sem=a_recv.at[off - 1],
            device_id=(node, peer), device_id_type=MESH,
        ))
    mine = pl.ds(node * CAP, CAP)
    copies += [
        pltpu.make_async_copy(terms_ref.at[mine], back_ref.at[mine], self_sem.at[0]),
        pltpu.make_async_copy(
            rows_ref.at[band(feat, depth)], activ_ref.at[:, band(feat, width)], self_sem.at[1]
        ),
    ]
    for copy in parts + copies:
        copy.start()

    for copy in parts:
        copy.wait()
    total = part_ref[feat].astype(jnp.float32)
    for i in range(feats - 1):
        total += feat_in[i].astype(jnp.float32)
    partial[...] = total.astype(jnp.bfloat16)
    slices = []
    for off in range(1, shards):
        peer = lax.rem(node + off, shards)
        slices.append(pltpu.make_async_remote_copy(
            src_ref=partial.at[peer], dst_ref=node_in.at[off - 1],
            send_sem=q_send.at[off - 1], recv_sem=q_recv.at[off - 1],
            device_id=(peer, feat), device_id_type=MESH,
        ))
    for copy in slices:
        copy.start()
    for copy in slices:
        copy.wait()
    total = partial[node].astype(jnp.float32)
    for i in range(shards - 1):
        total += node_in[i].astype(jnp.float32)
    reduced[...] = total.astype(jnp.bfloat16)
    spreads = []
    for off in range(1, shards):
        peer = lax.rem(node + off, shards)
        spreads.append(pltpu.make_async_remote_copy(
            src_ref=reduced, dst_ref=gathered.at[node],
            send_sem=r_send.at[off - 1], recv_sem=r_recv.at[off - 1],
            device_id=(peer, feat), device_id_type=MESH,
        ))
    for copy in spreads:
        copy.start()
    gathered[node] = reduced[...]
    for copy in spreads:
        copy.wait()
    grad_ref[...] = gathered[...].astype(jnp.float32) * scale
    for copy in copies:
        copy.wait()


def merge_kernel(shards, blocks, asked_ref, own_ref, back_ref, out_ref, acc):
    node = lax.axis_index("node")
    acc[...] = own_ref[...]
    for off in range(1, shards):
        peer = lax.rem(node + off, shards)

        @pl.loop(0, CAP)
        def _(k):
            acc[asked_ref[peer, k]] += back_ref[peer * CAP + k].astype(jnp.float32)

    for b in range(blocks):
        out_ref[:, b * LANES : (b + 1) * LANES] = acc[b].astype(jnp.bfloat16)


def per_device(shards, feats, x_feat, weight, out_grad, tile_rows, tile_cols, tile_masks):
    depth, local_rows = x_feat.shape
    blocks = local_rows // LANES
    tiles = tile_cols.shape[0]
    hidden = weight.shape[1]
    features = depth * feats
    per_feat = local_rows // feats
    slots = blocks + shards * CAP
    bf16, f32, i32 = jnp.bfloat16, jnp.float32, jnp.int32
    shape = jax.ShapeDtypeStruct
    dma = pltpu.SemaphoreType.DMA
    steps = tiles // GROUP

    asked, slot = pl.pallas_call(
        functools.partial(ask_kernel, shards, blocks),
        out_shape=(shape((shards, 1, LANES), i32), shape((1, tiles), i32)),
        in_specs=[spec(VMEM)],
        out_specs=(spec(VMEM), spec(VMEM)),
        scratch_shapes=[
            VMEM((shards, 1, LANES), i32), dma((shards - 1,)), dma((shards - 1,)), dma(()),
        ],
        compiler_params=params(16, collective_id=2, has_side_effects=True),
    )(tile_cols.reshape(1, tiles))
    asked, slot = asked.reshape(shards, LANES), slot.reshape(tiles)

    outbox = pl.pallas_call(
        functools.partial(pick_kernel, shards),
        out_shape=shape((shards * CAP, depth, LANES), bf16),
        in_specs=[spec(SMEM), spec(VMEM)],
        out_specs=spec(VMEM),
        compiler_params=params(24),
    )(asked, x_feat)

    source, cotangent_rows, full_weight, edges, turned = pl.pallas_call(
        functools.partial(fetch_kernel, shards, feats, blocks),
        out_shape=(
            shape((slots, depth, LANES), bf16),
            shape((features, per_feat), bf16),
            shape((features, hidden), bf16),
            shape((tiles, LANES, LANES), bf16),
            shape((tiles, LANES, LANES), bf16),
        ),
        in_specs=[spec(ANY)] * 5,
        out_specs=(spec(ANY),) * 5,
        scratch_shapes=[
            VMEM((tiles, LANES, LANES), i32),
            VMEM((tiles, LANES, LANES), bf16), VMEM((tiles, LANES, LANES), bf16), dma((3,)),
            dma((shards - 1,)), dma((shards - 1,)), dma((blocks,)),
            dma((feats - 1,)), dma((feats - 1,)), dma((feats - 1,)), dma((feats - 1,)),
            dma((3,)),
        ],
        compiler_params=params(40, collective_id=0, has_side_effects=True),
    )(outbox, x_feat, out_grad, weight, tile_masks)

    whole3 = lambda i, *_: (0, 0, 0)
    whole2 = lambda i, *_: (0, 0)
    by_tile = lambda i, *_: (i, 0, 0)
    aggregated, degree = pl.pallas_call(
        functools.partial(gather_kernel, steps, blocks),
        grid_spec=pltpu.PrefetchScalarGridSpec(
            num_scalar_prefetch=2,
            grid=(steps,),
            in_specs=[
                pl.BlockSpec((slots, depth, LANES), whole3),
                pl.BlockSpec((GROUP, LANES, LANES), by_tile),
            ],
            out_specs=(
                pl.BlockSpec((depth, local_rows), whole2),
                pl.BlockSpec((blocks, 1, LANES), whole3),
            ),
            scratch_shapes=[VMEM((blocks, depth + 16, LANES), f32)],
        ),
        out_shape=(
            shape((depth, local_rows), bf16),
            shape((blocks, 1, LANES), f32),
        ),
        compiler_params=params(40),
    )(tile_rows, slot, source, turned)

    parts = 2 if per_feat % (2 * LANES) == 0 else 1
    hidden_grad, row_activ, full_part = pl.pallas_call(
        functools.partial(dense_kernel, feats, parts),
        out_shape=(
            shape((depth, local_rows), bf16),
            shape((hidden, per_feat), bf16),
            shape((features, hidden), bf16),
        ),
        in_specs=[spec(ANY), spec(VMEM), spec(VMEM)],
        out_specs=(spec(ANY), spec(VMEM), spec(VMEM)),
        scratch_shapes=[
            VMEM((features, per_feat), bf16), VMEM((hidden, per_feat), bf16),
            VMEM((features, per_feat), bf16), VMEM((hidden, features), bf16),
            dma((parts, feats - 1)), dma((parts, feats - 1)),
            dma((parts, feats - 1)), dma((parts, feats - 1)), dma((2 * parts,)),
        ],
        compiler_params=params(32, collective_id=3, has_side_effects=True),
    )(aggregated, cotangent_rows, full_weight)
    slice_rows = depth // shards
    full_part = full_part.reshape(feats, shards, slice_rows, hidden)

    own, terms = pl.pallas_call(
        functools.partial(spread_kernel, steps, blocks),
        grid_spec=pltpu.PrefetchScalarGridSpec(
            num_scalar_prefetch=2,
            grid=(steps,),
            in_specs=[
                pl.BlockSpec((depth, local_rows), whole2),
                pl.BlockSpec((blocks, 1, LANES), whole3),
                pl.BlockSpec((GROUP, LANES, LANES), by_tile),
            ],
            out_specs=(
                pl.BlockSpec((blocks, depth, LANES), whole3),
                pl.BlockSpec((shards * CAP, depth, LANES), whole3),
            ),
            scratch_shapes=[
                VMEM((slots, depth, LANES), f32),
                VMEM((blocks, depth, LANES), bf16),
            ],
        ),
        out_shape=(
            shape((blocks, depth, LANES), f32),
            shape((shards * CAP, depth, LANES), bf16),
        ),
        compiler_params=params(40),
    )(tile_rows, slot, hidden_grad, degree, edges)

    piece = (slice_rows, hidden)
    back, activ, weight_grad = pl.pallas_call(
        functools.partial(return_kernel, shards, feats, (local_rows * shards) ** (-0.5)),
        out_shape=(
            shape((shards * CAP, depth, LANES), bf16),
            shape((depth, local_rows), bf16),
            shape((shards, *piece), f32),
        ),
        in_specs=[spec(ANY), spec(ANY), spec(VMEM)],
        out_specs=(spec(ANY), spec(ANY), spec(VMEM)),
        scratch_shapes=[
            VMEM((feats - 1, shards, *piece), bf16), VMEM((shards, *piece), bf16),
            VMEM((shards - 1, *piece), bf16), VMEM(piece, bf16), VMEM((shards, *piece), bf16),
            dma((shards - 1,)), dma((shards - 1,)), dma((feats - 1,)), dma((feats - 1,)), dma((2,)),
            dma((feats - 1,)), dma((feats - 1,)), dma((shards - 1,)), dma((shards - 1,)),
            dma((shards - 1,)), dma((shards - 1,)),
        ],
        compiler_params=params(24, collective_id=1, has_side_effects=True),
    )(terms, row_activ, full_part)
    weight_grad = weight_grad.reshape(depth, hidden)

    x_grad = pl.pallas_call(
        functools.partial(merge_kernel, shards, blocks),
        out_shape=shape((depth, local_rows), bf16),
        in_specs=[spec(SMEM), spec(VMEM), spec(VMEM)],
        out_specs=spec(VMEM),
        scratch_shapes=[VMEM((blocks, depth, LANES), f32)],
        compiler_params=params(32),
    )(asked, own, back)
    return (activ, x_grad, weight_grad)


def solution(mesh):
    placed = (
        P("feat", "node"),
        P("feat", None),
        P("feat", "node"),
        P("node"),
        P("node"),
        P("node", None, None),
    )
    return jax.shard_map(
        functools.partial(per_device, mesh.shape["node"], mesh.shape["feat"]),
        mesh=mesh,
        in_specs=placed,
        out_specs=(P("feat", "node"), P("feat", "node"), P("feat", None)),
        check_vma=False,
    )
```

```python
import functools

import jax
import jax.numpy as jnp
from jax import lax
from jax.experimental import pallas as pl
from jax.experimental.pallas import tpu as pltpu
from jax.sharding import PartitionSpec as P

CAP = 8
GROUP = 8
LANES = 128
MESH = pl.DeviceIdType.MESH
VMEM = pltpu.VMEM
SMEM = pltpu.SMEM
ANY = pl.ANY


def spec(space):
    return pl.BlockSpec(memory_space=space)


def params(limit_mib, **more):
    return pltpu.CompilerParams(vmem_limit_bytes=limit_mib << 20, **more)


def barrier(shards, feats):
    node, feat = lax.axis_index("node"), lax.axis_index("feat")
    sem = pltpu.get_barrier_semaphore()
    for off in range(1, shards):
        pl.semaphore_signal(
            sem, inc=1, device_id=(lax.rem(node + off, shards), feat), device_id_type=MESH
        )
    for off in range(1, feats):
        pl.semaphore_signal(
            sem, inc=1, device_id=(node, lax.rem(feat + off, feats)), device_id_type=MESH
        )
    pl.semaphore_wait(sem, max(shards - 1, 0) + max(feats - 1, 0))


def ask_kernel(
    shards, blocks, cols_ref, asked_ref, slot_ref, need, send_sem, recv_sem, self_sem
):
    node, feat = lax.axis_index("node"), lax.axis_index("feat")
    barrier(shards, 0)
    columns, tiles = shards * blocks, cols_ref.shape[1]
    f32, bf16 = jnp.float32, jnp.bfloat16

    def iota(dims, axis):
        return lax.broadcasted_iota(jnp.int32, dims, axis)

    def contract_columns(left, right):
        return lax.dot_general(left, right, (((0,), (0,)), ((), ())), preferred_element_type=f32)

    hits = (iota((columns, tiles), 0) == cols_ref[...]).astype(f32)
    present = jnp.minimum(jnp.sum(hits, axis=1, keepdims=True), 1.0)
    present = jnp.broadcast_to(present, (columns, LANES))
    below, above = iota((columns, columns), 0), iota((columns, columns), 1)
    earlier = ((below < above) & (below // blocks == above // blocks)).astype(f32).astype(bf16)
    order = contract_columns(earlier, present.astype(bf16))
    column, lane = iota((columns, LANES), 0), iota((columns, LANES), 1)
    shard = column // blocks
    local = (column - shard * blocks).astype(f32)
    chosen = jnp.where(order == lane.astype(f32), present * local, 0.0).astype(bf16)
    of_shard = (iota((columns, LANES), 0) // blocks == iota((columns, LANES), 1)).astype(f32)
    lists = contract_columns(of_shard.astype(bf16), chosen).astype(jnp.int32)
    for s in range(shards):
        need[s] = lists[s : s + 1]
    copies = []
    for off in range(1, shards):
        peer = lax.rem(node + off, shards)
        copy = pltpu.make_async_remote_copy(
            src_ref=need.at[peer], dst_ref=asked_ref.at[node],
            send_sem=send_sem.at[off - 1], recv_sem=recv_sem.at[off - 1],
            device_id=(peer, feat), device_id_type=MESH,
        )
        copy.start()
        copies.append(copy)
    own = pltpu.make_async_copy(need.at[node], asked_ref.at[node], self_sem)
    own.start()
    away = order + (shard * CAP + blocks).astype(f32)
    place = jnp.where(shard == node, local, jnp.minimum(away, 255.0)).astype(bf16)
    slot_ref[...] = contract_columns(place, hits.astype(bf16))[:1].astype(jnp.int32)
    own.wait()
    for copy in copies:
        copy.wait()


def pick_kernel(shards, asked_ref, x_ref, outbox_ref):
    for s in range(shards):

        @pl.loop(0, CAP)
        def _(k):
            columns = pl.ds(pl.multiple_of(asked_ref[s, k] * LANES, LANES), LANES)
            outbox_ref[s * CAP + k] = x_ref[:, columns]


def fetch_kernel(
    shards, feats, blocks, outbox_ref, x_ref, grad_ref, weight_ref, mask_ref, source_ref,
    cot_ref, full_ref, edge_ref, turned_ref, masks, edges, turned, mask_sem, x_send, x_recv, own_sem, cot_send, cot_recv, w_send, w_recv, self_sem,
):
    node, feat = lax.axis_index("node"), lax.axis_index("feat")
    depth = x_ref.shape[0]
    per_feat = cot_ref.shape[1]
    barrier(shards, feats)
    mine = pl.ds(node * CAP, CAP)
    landing = pl.ds(blocks + node * CAP, CAP)

    copies = []
    for off in range(1, shards):
        peer = lax.rem(node + off, shards)
        copies.append(pltpu.make_async_remote_copy(
            src_ref=outbox_ref.at[pl.ds(peer * CAP, CAP)], dst_ref=source_ref.at[landing],
            send_sem=x_send.at[off - 1], recv_sem=x_recv.at[off - 1],
            device_id=(peer, feat), device_id_type=MESH,
        ))
    rows = pl.ds(pl.multiple_of(feat * depth, depth), depth)
    for off in range(1, feats):
        peer = lax.rem(feat + off, feats)
        columns = pl.ds(pl.multiple_of(peer * per_feat, per_feat), per_feat)
        for src, dst, sent, got in (
            (weight_ref, full_ref.at[rows], w_send, w_recv),
            (grad_ref.at[:, columns], cot_ref.at[rows], cot_send, cot_recv),
        ):
            copies.append(pltpu.make_async_remote_copy(
                src_ref=src, dst_ref=dst, send_sem=sent.at[off - 1], recv_sem=got.at[off - 1],
                device_id=(node, peer), device_id_type=MESH,
            ))
    own = pl.ds(pl.multiple_of(feat * per_feat, per_feat), per_feat)
    copies += [
        pltpu.make_async_copy(weight_ref, full_ref.at[rows], self_sem.at[0]),
        pltpu.make_async_copy(grad_ref.at[:, own], cot_ref.at[rows], self_sem.at[1]),
        pltpu.make_async_copy(outbox_ref.at[mine], source_ref.at[landing], self_sem.at[2]),
    ]
    for b in range(blocks):
        copies.append(pltpu.make_async_copy(
            x_ref.at[:, pl.ds(b * LANES, LANES)], source_ref.at[b], own_sem.at[b]
        ))
    load = pltpu.make_async_copy(mask_ref, masks, mask_sem.at[0])
    load.start()
    for copy in copies:
        copy.start()
    load.wait()

    @pl.loop(0, masks.shape[0] // GROUP)
    def _(i):
        for g in range(GROUP):
            value = masks[i * GROUP + g].astype(jnp.float32)
            edges[i * GROUP + g] = value.astype(jnp.bfloat16)
            turned[i * GROUP + g] = value.T.astype(jnp.bfloat16)

    stores = [
        pltpu.make_async_copy(edges, edge_ref, mask_sem.at[1]),
        pltpu.make_async_copy(turned, turned_ref, mask_sem.at[2]),
    ]
    for copy in stores:
        copy.start()
    for copy in stores + copies:
        copy.wait()


def gather_kernel(steps, blocks, rows_ref, slot_ref, source_ref, turned_ref, agg_ref, deg_ref, acc):
    step = pl.program_id(0)
    depth = source_ref.shape[1]
    ones = jnp.ones((16, LANES), jnp.bfloat16)

    def term(g):
        t = step * GROUP + g
        source = jnp.concatenate([source_ref[slot_ref[t]], ones], axis=0)
        return rows_ref[t], jnp.dot(source, turned_ref[g], preferred_element_type=jnp.float32)

    @pl.when(step < blocks // GROUP)
    def _():
        for g in range(GROUP):
            row, value = term(g)
            acc[row] = value

    @pl.when(step >= blocks // GROUP)
    def _():
        for g in range(0, GROUP, 2):
            row0, value0 = term(g)
            row1, value1 = term(g + 1)
            acc[row0] += value0
            acc[row1] += value1

    @pl.when(step == steps - 1)
    def _():
        for b in range(blocks):
            degree = 1.0 + acc[b, depth : depth + 1, :]
            mixed = source_ref[b].astype(jnp.float32) + acc[b, :depth, :]
            agg_ref[:, b * LANES : (b + 1) * LANES] = (mixed / degree).astype(jnp.bfloat16)
            deg_ref[b] = degree


def spread_kernel(steps, blocks, rows_ref, slot_ref, hidden_ref, deg_ref, edge_ref, own_ref, terms_ref, acc, scaled):
    step = pl.program_id(0)

    @pl.when(step == 0)
    def _():
        for b in range(blocks):
            value = hidden_ref[:, b * LANES : (b + 1) * LANES].astype(jnp.float32) / deg_ref[b]
            value = value.astype(jnp.bfloat16)
            scaled[b] = value
            acc[b] = value.astype(jnp.float32)
        acc[blocks:] = jnp.zeros_like(acc[blocks:])

    def term(g):
        t = step * GROUP + g
        return slot_ref[t], jnp.dot(
            scaled[rows_ref[t]], edge_ref[g], preferred_element_type=jnp.float32
        )

    for g in range(0, GROUP, 2):
        slot0, value0 = term(g)
        slot1, value1 = term(g + 1)
        acc[slot0] += value0
        acc[slot1] += value1

    @pl.when(step == steps - 1)
    def _():
        own_ref[...] = acc[:blocks]
        terms_ref[...] = acc[blocks:].astype(jnp.bfloat16)


def band(index, size):
    return pl.ds(pl.multiple_of(index * size, size), size)


def dense_kernel(
    feats, parts, agg_ref, cot_ref, weight_ref, hidden_ref, activ_ref, part_ref,
    nodes, grads, outgoing, turned, in_send, in_recv, out_send, out_recv, self_sem,
):
    node, feat = lax.axis_index("node"), lax.axis_index("feat")
    depth = agg_ref.shape[0]
    per_feat = nodes.shape[1]
    width = per_feat // parts
    barrier(0, feats)
    arrivals, selfs = [], []
    for c in range(parts):
        here = pl.ds(c * width, width)
        arrivals.append([])
        for off in range(1, feats):
            peer = lax.rem(feat + off, feats)
            columns = pl.ds(pl.multiple_of(peer * per_feat + c * width, width), width)
            arrivals[c].append(pltpu.make_async_remote_copy(
                src_ref=agg_ref.at[:, columns], dst_ref=nodes.at[band(feat, depth), here],
                send_sem=in_send.at[c, off - 1], recv_sem=in_recv.at[c, off - 1],
                device_id=(node, peer), device_id_type=MESH,
            ))
        columns = pl.ds(pl.multiple_of(feat * per_feat + c * width, width), width)
        selfs.append(pltpu.make_async_copy(
            agg_ref.at[:, columns], nodes.at[band(feat, depth), here], self_sem.at[c]
        ))
    for c in range(parts):
        for copy in arrivals[c] + [selfs[c]]:
            copy.start()
    turned[...] = weight_ref[...].astype(jnp.float32).T.astype(jnp.bfloat16)
    returns = []
    for c in range(parts):
        for copy in arrivals[c] + [selfs[c]]:
            copy.wait()

        @pl.loop(0, width // LANES)
        def _(i):
            columns = pl.ds(pl.multiple_of(c * width + i * LANES, LANES), LANES)
            preact = jnp.dot(turned[...], nodes[:, columns], preferred_element_type=jnp.float32)
            sig = jax.nn.sigmoid(preact)
            activ_ref[:, columns] = (preact * sig).astype(jnp.bfloat16)
            slope = sig * (1.0 + preact * (1.0 - sig))
            grad = (cot_ref[:, columns].astype(jnp.float32) * slope).astype(jnp.bfloat16)
            grads[:, columns] = grad
            outgoing[:, columns] = jnp.dot(
                weight_ref[...], grad, preferred_element_type=jnp.float32
            ).astype(jnp.bfloat16)

        here = pl.ds(c * width, width)
        columns = pl.ds(pl.multiple_of(feat * per_feat + c * width, width), width)
        for off in range(1, feats):
            peer = lax.rem(feat + off, feats)
            returns.append(pltpu.make_async_remote_copy(
                src_ref=outgoing.at[band(peer, depth), here], dst_ref=hidden_ref.at[:, columns],
                send_sem=out_send.at[c, off - 1], recv_sem=out_recv.at[c, off - 1],
                device_id=(node, peer), device_id_type=MESH,
            ))
            returns[-1].start()
        returns.append(pltpu.make_async_copy(
            outgoing.at[band(feat, depth), here], hidden_ref.at[:, columns], self_sem.at[parts + c]
        ))
        returns[-1].start()

    @pl.loop(0, part_ref.shape[0] // LANES)
    def _(i):
        rows = pl.ds(pl.multiple_of(i * LANES, LANES), LANES)
        part_ref[rows] = lax.dot_general(
            nodes[rows], grads[...], (((1,), (1,)), ((), ())), preferred_element_type=jnp.float32
        ).astype(jnp.bfloat16)

    for copy in returns:
        copy.wait()


def return_kernel(
    shards, feats, scale, terms_ref, rows_ref, part_ref, back_ref, activ_ref, grad_ref,
    feat_in, partial, node_in, reduced, gathered, z_send, z_recv, a_send, a_recv, self_sem,
    p_send, p_recv, q_send, q_recv, r_send, r_recv,
):
    node, feat = lax.axis_index("node"), lax.axis_index("feat")
    depth = activ_ref.shape[0]
    width = rows_ref.shape[1]
    barrier(shards, feats)

    parts = []
    for off in range(1, feats):
        peer = lax.rem(feat + off, feats)
        parts.append(pltpu.make_async_remote_copy(
            src_ref=part_ref.at[peer], dst_ref=feat_in.at[off - 1],
            send_sem=p_send.at[off - 1], recv_sem=p_recv.at[off - 1],
            device_id=(node, peer), device_id_type=MESH,
        ))
    copies = []
    for off in range(1, shards):
        peer = lax.rem(node + off, shards)
        copies.append(pltpu.make_async_remote_copy(
            src_ref=terms_ref.at[pl.ds(peer * CAP, CAP)],
            dst_ref=back_ref.at[pl.ds(node * CAP, CAP)],
            send_sem=z_send.at[off - 1], recv_sem=z_recv.at[off - 1],
            device_id=(peer, feat), device_id_type=MESH,
        ))
    for off in range(1, feats):
        peer = lax.rem(feat + off, feats)
        copies.append(pltpu.make_async_remote_copy(
            src_ref=rows_ref.at[band(peer, depth)], dst_ref=activ_ref.at[:, band(feat, width)],
            send_sem=a_send.at[off - 1], recv_sem=a_recv.at[off - 1],
            device_id=(node, peer), device_id_type=MESH,
        ))
    mine = pl.ds(node * CAP, CAP)
    copies += [
        pltpu.make_async_copy(terms_ref.at[mine], back_ref.at[mine], self_sem.at[0]),
        pltpu.make_async_copy(
            rows_ref.at[band(feat, depth)], activ_ref.at[:, band(feat, width)], self_sem.at[1]
        ),
    ]
    for copy in parts + copies:
        copy.start()

    for copy in parts:
        copy.wait()
    total = part_ref[feat].astype(jnp.float32)
    for i in range(feats - 1):
        total += feat_in[i].astype(jnp.float32)
    partial[...] = total.astype(jnp.bfloat16)
    slices = []
    for off in range(1, shards):
        peer = lax.rem(node + off, shards)
        slices.append(pltpu.make_async_remote_copy(
            src_ref=partial.at[peer], dst_ref=node_in.at[off - 1],
            send_sem=q_send.at[off - 1], recv_sem=q_recv.at[off - 1],
            device_id=(peer, feat), device_id_type=MESH,
        ))
    for copy in slices:
        copy.start()
    for copy in slices:
        copy.wait()
    total = partial[node].astype(jnp.float32)
    for i in range(shards - 1):
        total += node_in[i].astype(jnp.float32)
    reduced[...] = total.astype(jnp.bfloat16)
    spreads = []
    for off in range(1, shards):
        peer = lax.rem(node + off, shards)
        spreads.append(pltpu.make_async_remote_copy(
            src_ref=reduced, dst_ref=gathered.at[node],
            send_sem=r_send.at[off - 1], recv_sem=r_recv.at[off - 1],
            device_id=(peer, feat), device_id_type=MESH,
        ))
    for copy in spreads:
        copy.start()
    gathered[node] = reduced[...]
    for copy in spreads:
        copy.wait()
    grad_ref[...] = gathered[...].astype(jnp.float32) * scale
    for copy in copies:
        copy.wait()


def merge_kernel(shards, blocks, asked_ref, own_ref, back_ref, out_ref, acc):
    node = lax.axis_index("node")
    acc[...] = own_ref[...]
    for off in range(1, shards):
        peer = lax.rem(node + off, shards)

        @pl.loop(0, CAP)
        def _(k):
            acc[asked_ref[peer, k]] += back_ref[peer * CAP + k].astype(jnp.float32)

    for b in range(blocks):
        out_ref[:, b * LANES : (b + 1) * LANES] = acc[b].astype(jnp.bfloat16)


def per_device(shards, feats, x_feat, weight, out_grad, tile_rows, tile_cols, tile_masks):
    depth, local_rows = x_feat.shape
    blocks = local_rows // LANES
    tiles = tile_cols.shape[0]
    hidden = weight.shape[1]
    features = depth * feats
    per_feat = local_rows // feats
    slots = blocks + shards * CAP
    bf16, f32, i32 = jnp.bfloat16, jnp.float32, jnp.int32
    shape = jax.ShapeDtypeStruct
    dma = pltpu.SemaphoreType.DMA
    steps = tiles // GROUP

    asked, slot = pl.pallas_call(
        functools.partial(ask_kernel, shards, blocks),
        out_shape=(shape((shards, 1, LANES), i32), shape((1, tiles), i32)),
        in_specs=[spec(VMEM)],
        out_specs=(spec(VMEM), spec(VMEM)),
        scratch_shapes=[
            VMEM((shards, 1, LANES), i32), dma((shards - 1,)), dma((shards - 1,)), dma(()),
        ],
        compiler_params=params(8, collective_id=2, has_side_effects=True),
    )(tile_cols.reshape(1, tiles))
    asked, slot = asked.reshape(shards, LANES), slot.reshape(tiles)

    outbox = pl.pallas_call(
        functools.partial(pick_kernel, shards),
        out_shape=shape((shards * CAP, depth, LANES), bf16),
        in_specs=[spec(SMEM), spec(VMEM)],
        out_specs=spec(VMEM),
        compiler_params=params(10),
    )(asked, x_feat)

    source, cotangent_rows, full_weight, edges, turned = pl.pallas_call(
        functools.partial(fetch_kernel, shards, feats, blocks),
        out_shape=(
            shape((slots, depth, LANES), bf16),
            shape((features, per_feat), bf16),
            shape((features, hidden), bf16),
            shape((tiles, LANES, LANES), bf16),
            shape((tiles, LANES, LANES), bf16),
        ),
        in_specs=[spec(ANY)] * 5,
        out_specs=(spec(ANY),) * 5,
        scratch_shapes=[
            VMEM((tiles, LANES, LANES), i32),
            VMEM((tiles, LANES, LANES), bf16), VMEM((tiles, LANES, LANES), bf16), dma((3,)),
            dma((shards - 1,)), dma((shards - 1,)), dma((blocks,)),
            dma((feats - 1,)), dma((feats - 1,)), dma((feats - 1,)), dma((feats - 1,)),
            dma((3,)),
        ],
        compiler_params=params(tiles // 8 + 5, collective_id=0, has_side_effects=True),
    )(outbox, x_feat, out_grad, weight, tile_masks)

    whole3 = lambda i, *_: (0, 0, 0)
    whole2 = lambda i, *_: (0, 0)
    by_tile = lambda i, *_: (i, 0, 0)
    aggregated, degree = pl.pallas_call(
        functools.partial(gather_kernel, steps, blocks),
        grid_spec=pltpu.PrefetchScalarGridSpec(
            num_scalar_prefetch=2,
            grid=(steps,),
            in_specs=[
                pl.BlockSpec((slots, depth, LANES), whole3),
                pl.BlockSpec((GROUP, LANES, LANES), by_tile),
            ],
            out_specs=(
                pl.BlockSpec((depth, local_rows), whole2),
                pl.BlockSpec((blocks, 1, LANES), whole3),
            ),
            scratch_shapes=[VMEM((blocks, depth + 16, LANES), f32)],
        ),
        out_shape=(
            shape((depth, local_rows), bf16),
            shape((blocks, 1, LANES), f32),
        ),
        compiler_params=params(16),
    )(tile_rows, slot, source, turned)

    parts = 2 if per_feat % (2 * LANES) == 0 else 1
    hidden_grad, row_activ, full_part = pl.pallas_call(
        functools.partial(dense_kernel, feats, parts),
        out_shape=(
            shape((depth, local_rows), bf16),
            shape((hidden, per_feat), bf16),
            shape((features, hidden), bf16),
        ),
        in_specs=[spec(ANY), spec(VMEM), spec(VMEM)],
        out_specs=(spec(ANY), spec(VMEM), spec(VMEM)),
        scratch_shapes=[
            VMEM((features, per_feat), bf16), VMEM((hidden, per_feat), bf16),
            VMEM((features, per_feat), bf16), VMEM((hidden, features), bf16),
            dma((parts, feats - 1)), dma((parts, feats - 1)),
            dma((parts, feats - 1)), dma((parts, feats - 1)), dma((2 * parts,)),
        ],
        compiler_params=params(16, collective_id=3, has_side_effects=True),
    )(aggregated, cotangent_rows, full_weight)
    slice_rows = depth // shards
    full_part = full_part.reshape(feats, shards, slice_rows, hidden)

    own, terms = pl.pallas_call(
        functools.partial(spread_kernel, steps, blocks),
        grid_spec=pltpu.PrefetchScalarGridSpec(
            num_scalar_prefetch=2,
            grid=(steps,),
            in_specs=[
                pl.BlockSpec((depth, local_rows), whole2),
                pl.BlockSpec((blocks, 1, LANES), whole3),
                pl.BlockSpec((GROUP, LANES, LANES), by_tile),
            ],
            out_specs=(
                pl.BlockSpec((blocks, depth, LANES), whole3),
                pl.BlockSpec((shards * CAP, depth, LANES), whole3),
            ),
            scratch_shapes=[
                VMEM((slots, depth, LANES), f32),
                VMEM((blocks, depth, LANES), bf16),
            ],
        ),
        out_shape=(
            shape((blocks, depth, LANES), f32),
            shape((shards * CAP, depth, LANES), bf16),
        ),
        compiler_params=params(24),
    )(tile_rows, slot, hidden_grad, degree, edges)

    piece = (slice_rows, hidden)
    back, activ, weight_grad = pl.pallas_call(
        functools.partial(return_kernel, shards, feats, (local_rows * shards) ** (-0.5)),
        out_shape=(
            shape((shards * CAP, depth, LANES), bf16),
            shape((depth, local_rows), bf16),
            shape((shards, *piece), f32),
        ),
        in_specs=[spec(ANY), spec(ANY), spec(VMEM)],
        out_specs=(spec(ANY), spec(ANY), spec(VMEM)),
        scratch_shapes=[
            VMEM((feats - 1, shards, *piece), bf16), VMEM((shards, *piece), bf16),
            VMEM((shards - 1, *piece), bf16), VMEM(piece, bf16), VMEM((shards, *piece), bf16),
            dma((shards - 1,)), dma((shards - 1,)), dma((feats - 1,)), dma((feats - 1,)), dma((2,)),
            dma((feats - 1,)), dma((feats - 1,)), dma((shards - 1,)), dma((shards - 1,)),
            dma((shards - 1,)), dma((shards - 1,)),
        ],
        compiler_params=params(8, collective_id=1, has_side_effects=True),
    )(terms, row_activ, full_part)
    weight_grad = weight_grad.reshape(depth, hidden)

    x_grad = pl.pallas_call(
        functools.partial(merge_kernel, shards, blocks),
        out_shape=shape((depth, local_rows), bf16),
        in_specs=[spec(SMEM), spec(VMEM), spec(VMEM)],
        out_specs=spec(VMEM),
        scratch_shapes=[VMEM((blocks, depth, LANES), f32)],
        compiler_params=params(32),
    )(asked, own, back)
    return (activ, x_grad, weight_grad)


def solution(mesh):
    placed = (
        P("feat", "node"),
        P("feat", None),
        P("feat", "node"),
        P("node"),
        P("node"),
        P("node", None, None),
    )
    return jax.shard_map(
        functools.partial(per_device, mesh.shape["node"], mesh.shape["feat"]),
        mesh=mesh,
        in_specs=placed,
        out_specs=(P("feat", "node"), P("feat", "node"), P("feat", None)),
        check_vma=False,
    )
```
